512 devices in a mesh: rep: 32 (over z, x_lo), gz: 16 (over x_hi, y, core).
Axes of the slice: x: 4 (x_hi: 2, x_lo: 2; x = x_hi * 2 + x_lo), y: 4, z: 16, core: 2. Of those that a mesh axis runs over, the one named last changes fastest.
Arguments:
- lattice_field: float32 [192, 64, 4096], P('rep', 'gz'), may hold values from -4 to 4
- langevin_noise: float32 [2, 192, 64, 4096], P(None, 'rep', 'gz'), may hold values from -5 to 5
- masses: float32 [64, 4096], P('gz'), may hold values from -2 to 2
- counts: int32 [192], replicated, may hold values from 0 to 49, as said below
- dest_slots: int32 [192], replicated, may hold values from 0 to 191, each once
- mode_bins: int32 [64, 64, 33], P('gz'), may hold values from 0 to 15, as said below
Outputs:
- resampled: float32 [192, 64, 4096], P('rep', 'gz')
- propagator: float32 [192, 16], P('rep')
The draws below stay inside these ranges and needn't reach their ends.
Inputs may be any that keep to these rules, and one draw needn't show every extreme that they name: The counts sum to 192; in each aligned block of 6 replicas (those of one index of rep) at most 3 counts are nonzero, and exactly 3 in some block. `dest_slots`: A permutation of the 192 slots. `mode_bins`: the bin depends only on n_y^2 + n_z^2 + kx^2 with n = min(k, 64 - k), and never falls as that grows; every bin holds at least one mode.
All inputs are finite; a program needn't handle non-finite values.
Results may differ from the reference program's by a relative error of at most 0.00007.
Values sent between devices are 32-bit elements; how exact they have to be, the bound alone decides.
No kernel may reach another device: no remote copies, remote signals or barrier semaphores. Data moves between devices by JAX's collectives and lax.ppermute only.
A program may use at most 64 MiB of HBM per device.

```python
import jax
import jax.numpy as jnp
from jax import lax

L = 64
REP_DEV = 6
SWEEPS = 2
NBINS = 16
LIVE_DEV = 3
REPLICAS = 192


def draw_counts(key, part):
    subkeys = jax.random.split(key, 4)
    blocks = REPLICAS // REP_DEV
    least = max((LIVE_DEV + 1) // 2, 1)
    live_number = jax.random.randint(subkeys[0], (blocks,), least, LIVE_DEV + 1)
    chosen = jax.random.randint(subkeys[1], (), 0, blocks)
    live_number = jnp.where(jnp.arange(blocks) == chosen, LIVE_DEV, live_number)
    scores = jax.random.randint(subkeys[2], (blocks, REP_DEV), 0, 1 << 20) * REP_DEV + jnp.arange(REP_DEV)[None, :]
    ranking = jnp.argsort(jnp.argsort(scores, axis=1), axis=1)
    alive = (ranking < live_number[:, None]).reshape(REPLICAS).astype(jnp.int32)
    total_live = jnp.sum(alive)
    live_first = jnp.argsort(1 - alive, stable=True)
    big_extra = REPLICAS // 4
    second_extra = REPLICAS // 8
    big_index = jax.random.randint(subkeys[3], (), 0, 1 << 20) % total_live
    second_index = (big_index + 1) % total_live
    remaining = REPLICAS - total_live - big_extra - second_extra
    others = total_live - 2
    turns = jnp.arange(REPLICAS)
    spots = (big_index + 2 + turns // 3 % others) % total_live
    target = live_first[spots]
    extra = (turns < remaining).astype(jnp.int32)
    spread = jnp.zeros((REPLICAS,), jnp.int32).at[target].add(extra)
    big_add = jnp.zeros((REPLICAS,), jnp.int32).at[live_first[big_index]].add(big_extra)
    second_add = jnp.zeros((REPLICAS,), jnp.int32).at[live_first[second_index]].add(second_extra)
    return (alive + spread + big_add + second_add).astype(jnp.int32)


def draw_mode_bins(key, part):
    half = L // 2
    folded = jnp.minimum(jnp.arange(L), L - jnp.arange(L))
    wave_x = jnp.arange(half + 1)
    squared = folded[:, None, None] ** 2 + folded[None, :, None] ** 2 + wave_x[None, None, :] ** 2
    reach = half * half
    offsets = jnp.sort(jax.random.randint(key, (NBINS - 1,), 0, reach - 8 * NBINS))
    edges = 8 * jnp.arange(1, NBINS) + offsets
    return jnp.sum((squared[..., None] >= edges).astype(jnp.int32), axis=-1).astype(jnp.int32)


def levels(rng, dims, cuts, low, top_value):
    gain, own = 1.0, jax.random.fold_in(rng, 6)
    for axis_at, shards_of in cuts:
        heights = jnp.exp(jax.random.uniform(jax.random.fold_in(own, axis_at), (shards_of,), jnp.float32, low / len(cuts), top_value / len(cuts)))
        gain = gain * jnp.repeat(heights, dims[axis_at] // shards_of).reshape([-1 if axis == axis_at else 1 for axis in range(len(dims))])
    return gain


def noise(stream_key, extent, scale, bound, shards=(), held_as=jnp.bfloat16):
    level = levels(stream_key, extent, shards, -0.22, 0.18) if shards else 1.0
    array = jax.random.normal(stream_key, extent, jnp.float32) * scale * level
    return jnp.minimum(jnp.maximum(array, -bound), bound).astype(held_as)


def setup_inputs(seed: int = 0) -> dict:
    streams_of = jax.random.split(jax.random.key(seed), 7)
    return {
        "lattice_field": noise(streams_of[0], (REPLICAS, L, L * L), 1.0, 4.0, ((0, 32), (1, 16)), jnp.float32),
        "langevin_noise": noise(streams_of[1], (SWEEPS, REPLICAS, L, L * L), 1.0, 5.0, ((1, 32), (2, 16)), jnp.float32),
        "masses": jnp.clip(jax.random.uniform(streams_of[2], (L, L * L), jnp.float32, -2.0, 2.0) * levels(streams_of[2], (L, L * L), ((0, 16),), -0.4, 0.0), -2.0, 2.0),
        "counts": draw_counts(jax.random.fold_in(streams_of[6], 71), 0),
        "dest_slots": jax.random.permutation(streams_of[4], REPLICAS).astype(jnp.int32),
        "mode_bins": draw_mode_bins(jax.random.fold_in(streams_of[6], 71), 0),
    }


step_size = 0.1
quartic = 0.5

def sweep(field, noise_now, masses):
    plane = jnp.roll(field, 1, axis=1) + jnp.roll(field, -1, axis=1)
    grid = field.reshape(field.shape[0], L, L, L)
    inner = jnp.roll(grid, 1, axis=2) + jnp.roll(grid, -1, axis=2) + jnp.roll(grid, 1, axis=3) + jnp.roll(grid, -1, axis=3)
    beside = plane + inner.reshape(field.shape)
    drift = 6.0 * field - beside + masses[None] * field + quartic * field * field * field
    return field - step_size * drift + jnp.sqrt(2.0 * step_size) * noise_now

def sources(counts, dest_slots):
    ends = jnp.cumsum(counts).astype(jnp.int32)
    position = jnp.argsort(dest_slots).astype(jnp.int32)
    return lax.optimization_barrier(jnp.sum((ends[None, :] <= position[:, None]).astype(jnp.int32), axis=1)).astype(jnp.int32)

def mode_weights(mode_bins):
    ordered = jnp.transpose(mode_bins, (1, 0, 2))
    wave_x = jnp.arange(L // 2 + 1)
    weight_x = jnp.where((wave_x == 0) | (wave_x == L // 2), 1.0, 2.0).astype(jnp.float32)
    onehot = (ordered[..., None] == jnp.arange(NBINS)[None, None, None, :]).astype(jnp.float32)
    return (onehot * weight_x[None, None, :, None]).reshape(-1, NBINS)

def reference(lattice_field, langevin_noise, masses, counts, dest_slots, mode_bins):
    swept = lattice_field
    for turn in range(SWEEPS):
        swept = sweep(swept, langevin_noise[turn], masses)
    source = sources(counts, dest_slots)
    resampled = jnp.take(swept, source, axis=0)
    weights = mode_weights(mode_bins)

    def one_replica(replica):
        spectrum = jnp.fft.rfftn(replica.reshape(L, L, L))
        power = jnp.real(spectrum) ** 2 + jnp.imag(spectrum) ** 2
        return jnp.dot(power.reshape(1, -1), weights, precision=lax.Precision.HIGHEST)[0]
    binned = lax.map(one_replica, resampled)
    bin_weight = lax.optimization_barrier(jnp.sum(weights, axis=0))
    propagator = binned / (float(L ** 3) * bin_weight)
    return (resampled, propagator)
```

```python
import jax
import jax.numpy as jnp
import ml_dtypes
import numpy as np
from jax import lax
from jax.experimental import pallas as pl
from jax.experimental.pallas import tpu as pltpu
from jax.sharding import PartitionSpec as P

L = 64
NBINS = 16
LIVE = 3
DEPTH = 4
ROWS = 32
PER = 6

VMEM = pltpu.VMEM
SMEM = pltpu.SMEM


def split_constant(table):
    table = table.astype(np.float32)
    high = table.astype(ml_dtypes.bfloat16)
    low = (table - high.astype(np.float32)).astype(ml_dtypes.bfloat16)
    return np.stack([high, low])


def real_basis(sine_wave):
    slot = np.arange(L)[:, None]
    site = np.arange(L)[None, :]
    wave = np.where(slot <= L // 2, slot, sine_wave(slot))
    angle = 2.0 * np.pi / L * (wave * site % L)
    basis = np.where(slot <= L // 2, np.cos(angle), np.sin(angle)) * np.sqrt(2.0)
    basis[0] = 1.0
    basis[L // 2] = np.cos(np.pi * np.arange(L))
    return basis / np.sqrt(L)


def tables():
    basis_x = real_basis(lambda slot: slot - L // 2)
    basis_k = real_basis(lambda slot: L - slot)
    along_x = np.einsum("ab,cd,mx->acxdbm", np.eye(2), np.eye(2), basis_x).reshape(256, 256)
    along_y = basis_k.reshape(16, 2, 2, 32, 2).transpose(2, 1, 0, 4, 3).reshape(64, 64)
    along_z = np.einsum("ab,kz->akzb", np.eye(2), basis_k).reshape(128, 128)
    return split_constant(along_x), split_constant(along_y), split_constant(along_z)


def split(value):
    high = value.astype(jnp.bfloat16)
    return high, (value - high.astype(jnp.float32)).astype(jnp.bfloat16)


def dot(a, b):
    return jnp.dot(a, b, preferred_element_type=jnp.float32)


def live_of(counts_ref, base):
    seen = jnp.int32(0)
    live = [jnp.int32(0)] * LIVE
    for j in range(PER):
        alive = counts_ref[base + j] > 0
        for k in range(LIVE):
            live[k] = jnp.where(alive & (seen == k), j, live[k])
        seen = seen + alive.astype(jnp.int32)
    return live


def edges_kernel(base_ref, counts_ref, field, noise, masses, up, down, fbuf, nbuf, mbuf, sems):
    live = live_of(counts_ref, base_ref[0])
    copies = [pltpu.make_async_copy(masses, mbuf, sems.at[2 * LIVE])]
    for k in range(LIVE):
        copies.append(pltpu.make_async_copy(field.at[live[k]], fbuf.at[k], sems.at[2 * k]))
        copies.append(pltpu.make_async_copy(noise.at[0, live[k]], nbuf.at[k], sems.at[2 * k + 1]))
    for copy in copies:
        copy.start()
    for copy in copies:
        copy.wait()
    for k in range(LIVE):
        up[2 * k] = fbuf[k, pl.ds(2, ROWS, stride=DEPTH), :]
        up[2 * k + 1] = fbuf[k, pl.ds(3, ROWS, stride=DEPTH), :]
        down[2 * k] = fbuf[k, pl.ds(0, ROWS, stride=DEPTH), :]
        down[2 * k + 1] = fbuf[k, pl.ds(1, ROWS, stride=DEPTH), :]
        up[2 * LIVE + k] = nbuf[k, pl.ds(3, ROWS, stride=DEPTH), :]
        down[2 * LIVE + k] = nbuf[k, pl.ds(0, ROWS, stride=DEPTH), :]
    up[3 * LIVE] = mbuf[pl.ds(3, ROWS, stride=DEPTH), :]
    down[3 * LIVE] = mbuf[pl.ds(0, ROWS, stride=DEPTH), :]


def floor_div(value, by):
    return jnp.floor((value.astype(jnp.float32) + 0.5) * (1.0 / by)).astype(jnp.int32)


def plan_kernel(counts_ref, slots_ref, bins_ref, item_ref, wide_ref, map_ref):
    total = counts_ref.shape[1]
    row = lax.broadcasted_iota(jnp.int32, (total, total), 0)
    col = lax.broadcasted_iota(jnp.int32, (total, total), 1)
    number = jnp.broadcast_to(counts_ref[...].astype(jnp.float32), (total, total))
    slot = jnp.broadcast_to(slots_ref[...].astype(jnp.float32), (total, total))

    def along(mask, value):
        return jnp.sum(jnp.where(mask, value, 0.0), axis=1, keepdims=True)

    own = along(row == col, number)
    ends = along(col <= row, number)
    slot_column = along(row == col, slot)
    block_row = floor_div(row, PER)
    block_col = floor_div(col, PER)
    rank = along((block_row == block_col) & (col < row) & (number > 0.0), jnp.ones_like(number))
    name = rank + LIVE * block_row[:, :1].astype(jnp.float32)
    position = jnp.sum(
        jnp.where(slot_column == col.astype(jnp.float32), row.astype(jnp.float32), 0.0), axis=0, keepdims=True
    )
    held = (position >= ends - own) & (position < ends)
    item = jnp.sum(jnp.where(held, name, 0.0), axis=0, keepdims=True)
    item_ref[...] = item.astype(jnp.int32)
    devices = total // PER
    to = lax.broadcasted_iota(jnp.int32, (devices, total), 0)
    s = lax.broadcasted_iota(jnp.int32, (devices, total), 1)
    lane = lax.broadcasted_iota(jnp.int32, (devices, 128), 1)
    wide = jnp.full((devices, 128), -1.0, jnp.float32)
    items = jnp.broadcast_to(item, (devices, total))
    for q in range(PER):
        column = jnp.sum(jnp.where(s == to * PER + q, items, 0.0), axis=1, keepdims=True)
        wide = jnp.where((lane >= NBINS * q) & (lane < NBINS * (q + 1)), column, wide)
    wide_ref[...] = wide.astype(jnp.int32)
    lane = lax.broadcasted_iota(jnp.int32, (L, 128), 1)
    for pair in range(2):
        halves = []
        for odd in range(2):
            bins = bins_ref[2 * pair + odd]
            halves.append(jnp.where(lane <= L // 2, bins, pltpu.roll(bins, L // 2, axis=1)))
        map_ref[pair * L : (pair + 1) * L, :] = jnp.where(lane < L, halves[0], pltpu.roll(halves[1], L, axis=1))


def beside(v, lane):
    swapped = pltpu.roll(v, L, axis=1)
    rows = v.shape[0]
    y = swapped + jnp.where(lane < L, pltpu.roll(swapped, 1, axis=0), pltpu.roll(swapped, rows - 1, axis=0))
    inner = lane & (L - 1)
    low = pltpu.roll(jnp.where(inner == L - 1, swapped, v), 1, axis=1)
    high = pltpu.roll(jnp.where(inner == 0, swapped, v), 127, axis=1)
    return y + (low + high)


def sweep_kernel(
    base_ref, counts_ref, field, noise, masses, lo, hi, along_x, along_y, pieces, chunks, fbuf, nbuf, mbuf, sems
):
    live = live_of(counts_ref, base_ref[0])
    first = pltpu.make_async_copy(masses, mbuf, sems.at[3 * LIVE])
    first.start()
    copies = []
    for k in range(LIVE):
        copies.append(
            [
                pltpu.make_async_copy(field.at[live[k]], fbuf.at[k], sems.at[3 * k]),
                pltpu.make_async_copy(noise.at[0, live[k]], nbuf.at[0, k], sems.at[3 * k + 1]),
                pltpu.make_async_copy(noise.at[1, live[k]], nbuf.at[1, k], sems.at[3 * k + 2]),
            ]
        )
        for copy in copies[-1]:
            copy.start()
    first.wait()
    lane = lax.broadcasted_iota(jnp.int32, (ROWS, 128), 1)
    kick = float(np.sqrt(np.float32(0.2)))

    def update(center, below, above, mass, noise_now):
        near = below + above + beside(center, lane)
        return center * (0.4 - 0.1 * mass - 0.05 * (center * center)) + 0.1 * near + kick * noise_now

    def planes(ref, *at):
        return [ref[(*at, pl.ds(z, ROWS, stride=DEPTH), slice(None))] for z in range(DEPTH)]

    mass = [lo[3 * LIVE]] + planes(mbuf) + [hi[3 * LIVE]]
    left = []
    for k in range(LIVE):
        for copy in copies[k]:
            copy.wait()
        old = [lo[2 * k], lo[2 * k + 1]] + planes(fbuf, k) + [hi[2 * k], hi[2 * k + 1]]
        kicks = [lo[2 * LIVE + k]] + planes(nbuf, 0, k) + [hi[2 * LIVE + k]]
        mid = [update(old[p + 1], old[p], old[p + 2], mass[p], kicks[p]) for p in range(DEPTH + 2)]
        kicks = planes(nbuf, 1, k)
        new = [update(mid[p + 1], mid[p], mid[p + 2], mass[p + 1], kicks[p]) for p in range(DEPTH)]
        for z in range(DEPTH):
            pieces[pl.ds(k * DEPTH + z, ROWS, stride=LIVE * DEPTH), :] = new[z]
        left += [jnp.concatenate(new[0:2], axis=1), jnp.concatenate(new[2:4], axis=1)]
    high, low = split(jnp.concatenate(left, axis=0))
    across = dot(high, along_x[0]) + (dot(low, along_x[0]) + dot(high, along_x[1]))
    parts = [across[i * ROWS : (i + 1) * ROWS] for i in range(2 * LIVE)]
    right = jnp.concatenate([jnp.concatenate([p[:, :128], p[:, 128:]], axis=0) for p in parts], axis=1)
    high, low = split(right)
    turned = dot(along_y[0], high) + (dot(along_y[0], low) + dot(along_y[1], high))
    for i in range(2 * LIVE):
        even = turned[:ROWS, 128 * i : 128 * (i + 1)]
        odd = turned[ROWS:, 128 * i : 128 * (i + 1)]
        ready = (
            jnp.where(lane < L, even, pltpu.roll(odd, L, axis=1)),
            jnp.where(lane < L, pltpu.roll(even, L, axis=1), odd),
        )
        for side in range(2):
            for pair in range(2):
                chunks[pl.ds(i * 4 + side * 2 + pair, 16, stride=8 * LIVE), :] = ready[side][16 * pair : 16 * pair + 16]


def bins_kernel(chunks, map_ref, along_z, out, rows):
    place = map_ref[...]
    power = []
    for k in range(LIVE):
        high, low = split(chunks[:, 8 * k : 8 * k + 8, :].reshape(128, 128))
        mode = dot(along_z[0], high) + (dot(along_z[0], low) + dot(along_z[1], high))
        power.append(mode * mode)
    power.append(jnp.ones_like(power[0]))
    for b in range(NBINS):
        here = place == b
        for k in range(LIVE + 1):
            rows[k * NBINS + b : k * NBINS + b + 1, :] = jnp.sum(
                jnp.where(here, power[k], 0.0), axis=0, keepdims=True
            )
    rows[(LIVE + 1) * NBINS :, :] = jnp.zeros((128 - (LIVE + 1) * NBINS, 128), jnp.float32)
    sums = lax.dot_general(
        jnp.ones((8, 128), jnp.float32),
        rows[...],
        (((1,), (1,)), ((), ())),
        precision=lax.Precision.HIGHEST,
        preferred_element_type=jnp.float32,
    )
    for g in range(out.shape[0]):
        out[g] = sums[0:1]


def pick_kernel(item_ref, me_ref, pieces, sums, wide, out):
    total = item_ref.shape[0]
    devices = total // PER
    lane = lax.broadcasted_iota(jnp.int32, (1, 128), 1)
    summed = jnp.sum(sums[...].reshape(sums.shape[0], 128), axis=0, keepdims=True)

    def spread(k):
        v = jnp.where((lane >= NBINS * k) & (lane < NBINS * (k + 1)), summed, 0.0)
        for shift in (16, 32, 64):
            v = v + pltpu.roll(v, shift, axis=1)
        return v

    weight = spread(LIVE)
    mine = jnp.zeros((devices, 128), jnp.float32)
    for k in range(LIVE):
        mine = jnp.where(wide[...] == me_ref[0] * LIVE + k, spread(k) / weight, mine)
    for d in range(devices):
        for q in range(PER):
            out[d * (PER + 1) + q] = pieces[item_ref[d * PER + q]]
        out[d * (PER + 1) + PER] = jnp.broadcast_to(mine[d : d + 1], (DEPTH, 128))


def finish_kernel(got, resampled, propagator):
    devices = got.shape[0] // (PER + 1)
    sums = got[PER]
    for d in range(1, devices):
        sums = sums + got[d * (PER + 1) + PER]
    for q in range(PER):
        for d in range(devices):
            resampled[q, :, 128 * d : 128 * (d + 1)] = got[d * (PER + 1) + q]
    for q in range(PER):
        turned = sums if q == 0 else pltpu.roll(sums, 128 - NBINS * q, axis=1)
        propagator[q : q + 1, :] = turned[0:1, :NBINS]


def spec(space):
    return pl.BlockSpec(memory_space=space)


def shape(*dims, dtype=jnp.float32):
    return jax.ShapeDtypeStruct(dims, dtype)


def rows_view(slabs):
    lead = slabs.shape[:-2]
    parts = slabs.reshape(*lead, DEPTH, ROWS, 128)
    return jnp.swapaxes(parts, -3, -2).reshape(*lead, DEPTH * ROWS, 128)


def edges(base, counts, field, noise, masses):
    return pl.pallas_call(
        edges_kernel,
        out_shape=[shape(3 * LIVE + 1, ROWS, 128)] * 2,
        in_specs=[spec(SMEM)] * 2 + [spec(pl.ANY)] * 3,
        out_specs=[spec(VMEM)] * 2,
        scratch_shapes=[
            VMEM((LIVE, 128, 128), jnp.float32),
            VMEM((LIVE, 128, 128), jnp.float32),
            VMEM((128, 128), jnp.float32),
            pltpu.SemaphoreType.DMA((2 * LIVE + 1,)),
        ],
        name="edges",
    )(base, counts, field, noise, masses)


def plan(counts, dest_slots, mode_bins):
    total = counts.shape[0]
    padded = jnp.pad(mode_bins, ((0, 0), (0, 0), (0, 128 - mode_bins.shape[2])))
    return pl.pallas_call(
        plan_kernel,
        out_shape=[
            shape(1, total, dtype=jnp.int32),
            shape(total // PER, 128, dtype=jnp.int32),
            shape(128, 128, dtype=jnp.int32),
        ],
        in_specs=[spec(VMEM)] * 3,
        out_specs=[spec(VMEM)] * 3,
        name="plan",
    )(counts.reshape(1, total), dest_slots.reshape(1, total), padded)


def sweeps(base, counts, field, noise, masses, lo, hi, along_x, along_y):
    return pl.pallas_call(
        sweep_kernel,
        out_shape=[shape(ROWS * LIVE * DEPTH, 128), shape(16 * 8 * LIVE, 128)],
        in_specs=[spec(SMEM)] * 2 + [spec(pl.ANY)] * 3 + [spec(VMEM)] * 4,
        out_specs=[spec(VMEM)] * 2,
        scratch_shapes=[
            VMEM((LIVE, 128, 128), jnp.float32),
            VMEM((2, LIVE, 128, 128), jnp.float32),
            VMEM((128, 128), jnp.float32),
            pltpu.SemaphoreType.DMA((3 * LIVE + 1,)),
        ],
        name="sweeps",
    )(base, counts, field, noise, masses, lo, hi, along_x, along_y)


def bins(chunks, place, along_z):
    return pl.pallas_call(
        bins_kernel,
        out_shape=shape(16, 1, 128),
        in_specs=[spec(VMEM)] * 3,
        out_specs=spec(VMEM),
        scratch_shapes=[VMEM((128, 128), jnp.float32)],
        name="bins",
    )(chunks, place, along_z)


def pick(item, me, pieces, sums, wide):
    devices = item.shape[0] // PER
    return pl.pallas_call(
        pick_kernel,
        out_shape=shape(devices * (PER + 1), DEPTH, 128),
        in_specs=[spec(SMEM)] * 2 + [spec(VMEM)] * 3,
        out_specs=spec(VMEM),
        name="pick",
    )(item, me, pieces, sums, wide)


def finish(got):
    return pl.pallas_call(
        finish_kernel,
        out_shape=[shape(PER, DEPTH, L * L), shape(PER, NBINS)],
        in_specs=[spec(VMEM)],
        out_specs=[spec(VMEM)] * 2,
        name="finish",
    )(got)


def local(lattice_field, langevin_noise, masses, counts, dest_slots, mode_bins):
    along_x, along_y, along_z = (jnp.asarray(t) for t in tables())
    me = lax.axis_index("rep").astype(jnp.int32).reshape(1)
    base = me * PER
    field, noise, mass = rows_view(lattice_field), rows_view(langevin_noise), rows_view(masses)
    up, down = edges(base, counts, field, noise, mass)
    ring = lax.axis_size("gz")
    forward = [(i, (i + 1) % ring) for i in range(ring)]
    lo = lax.ppermute(up, "gz", forward)
    hi = lax.ppermute(down, "gz", [(b, a) for a, b in forward])
    item, wide, place = plan(counts, dest_slots, mode_bins)
    pieces, chunks = sweeps(base, counts, field, noise, mass, lo, hi, along_x, along_y)
    reps = lax.axis_size("rep")
    chunks = lax.all_to_all(chunks.reshape(ring, 8 * LIVE, 128), "gz", 0, 0, tiled=True)
    pieces = lax.all_to_all(pieces.reshape(reps, LIVE, DEPTH, 128), "rep", 0, 0, tiled=True)
    sums = lax.all_to_all(bins(chunks, place, along_z), "gz", 0, 0, tiled=True)
    out = pick(item.reshape(-1), me, pieces.reshape(reps * LIVE, DEPTH, 128), sums, wide)
    got = lax.all_to_all(out.reshape(reps, PER + 1, DEPTH, 128), "rep", 0, 0, tiled=True)
    resampled, propagator = finish(got.reshape(reps * (PER + 1), DEPTH, 128))
    return resampled, propagator


def solution(mesh):
    in_specs = (
        P("rep", "gz", None),
        P(None, "rep", "gz", None),
        P("gz", None),
        P(),
        P(),
        P("gz", None, None),
    )
    out_specs = (P("rep", "gz", None), P("rep", None))
    return jax.shard_map(local, mesh=mesh, in_specs=in_specs, out_specs=out_specs, check_vma=False)
```

```python
import jax
import jax.numpy as jnp
import ml_dtypes
import numpy as np
from jax import lax
from jax.experimental import pallas as pl
from jax.experimental.pallas import tpu as pltpu
from jax.sharding import PartitionSpec as P

L = 64
NBINS = 16
LIVE = 3
DEPTH = 4
ROWS = 32
PER = 6

VMEM = pltpu.VMEM
SMEM = pltpu.SMEM


def split_constant(table):
    table = table.astype(np.float32)
    high = table.astype(ml_dtypes.bfloat16)
    low = (table - high.astype(np.float32)).astype(ml_dtypes.bfloat16)
    return np.stack([high, low])


def real_basis(sine_wave):
    slot = np.arange(L)[:, None]
    site = np.arange(L)[None, :]
    wave = np.where(slot <= L // 2, slot, sine_wave(slot))
    angle = 2.0 * np.pi / L * (wave * site % L)
    basis = np.where(slot <= L // 2, np.cos(angle), np.sin(angle)) * np.sqrt(2.0)
    basis[0] = 1.0
    basis[L // 2] = np.cos(np.pi * np.arange(L))
    return basis / np.sqrt(L)


def tables():
    basis_x = real_basis(lambda slot: slot - L // 2)
    basis_k = real_basis(lambda slot: L - slot)
    along_x = np.einsum("ab,cd,mx->acxdbm", np.eye(2), np.eye(2), basis_x).reshape(256, 256)
    along_y = basis_k.reshape(16, 2, 2, 32, 2).transpose(2, 1, 0, 4, 3).reshape(64, 64)
    along_z = np.einsum("ab,kz->akzb", np.eye(2), basis_k).reshape(128, 128)
    return split_constant(along_x), split_constant(along_y), split_constant(along_z)


def split(value):
    high = value.astype(jnp.bfloat16)
    return high, (value - high.astype(jnp.float32)).astype(jnp.bfloat16)


def dot(a, b):
    return jnp.dot(a, b, preferred_element_type=jnp.float32)


def live_of(counts_ref, base):
    seen = jnp.int32(0)
    live = [jnp.int32(0)] * LIVE
    for j in range(PER):
        alive = counts_ref[base + j] > 0
        for k in range(LIVE):
            live[k] = jnp.where(alive & (seen == k), j, live[k])
        seen = seen + alive.astype(jnp.int32)
    return live


def edges_kernel(base_ref, counts_ref, field, noise, masses, up, down, fbuf, nbuf, mbuf, sems):
    live = live_of(counts_ref, base_ref[0])
    copies = [pltpu.make_async_copy(masses, mbuf, sems.at[2 * LIVE])]
    for k in range(LIVE):
        copies.append(pltpu.make_async_copy(field.at[live[k]], fbuf.at[k], sems.at[2 * k]))
        copies.append(pltpu.make_async_copy(noise.at[0, live[k]], nbuf.at[k], sems.at[2 * k + 1]))
    for copy in copies:
        copy.start()
    for copy in copies:
        copy.wait()
    for k in range(LIVE):
        up[2 * k] = fbuf[k, pl.ds(2, ROWS, stride=DEPTH), :]
        up[2 * k + 1] = fbuf[k, pl.ds(3, ROWS, stride=DEPTH), :]
        down[2 * k] = fbuf[k, pl.ds(0, ROWS, stride=DEPTH), :]
        down[2 * k + 1] = fbuf[k, pl.ds(1, ROWS, stride=DEPTH), :]
        up[2 * LIVE + k] = nbuf[k, pl.ds(3, ROWS, stride=DEPTH), :]
        down[2 * LIVE + k] = nbuf[k, pl.ds(0, ROWS, stride=DEPTH), :]
    up[3 * LIVE] = mbuf[pl.ds(3, ROWS, stride=DEPTH), :]
    down[3 * LIVE] = mbuf[pl.ds(0, ROWS, stride=DEPTH), :]


def floor_div(value, by):
    return jnp.floor((value.astype(jnp.float32) + 0.5) * (1.0 / by)).astype(jnp.int32)


def plan_kernel(counts_ref, slots_ref, bins_ref, item_ref, wide_ref, map_ref):
    total = counts_ref.shape[1]
    row = lax.broadcasted_iota(jnp.int32, (total, total), 0)
    col = lax.broadcasted_iota(jnp.int32, (total, total), 1)
    number = jnp.broadcast_to(counts_ref[...].astype(jnp.float32), (total, total))
    slot = jnp.broadcast_to(slots_ref[...].astype(jnp.float32), (total, total))

    def along(mask, value):
        return jnp.sum(jnp.where(mask, value, 0.0), axis=1, keepdims=True)

    own = along(row == col, number)
    ends = along(col <= row, number)
    slot_column = along(row == col, slot)
    block_row = floor_div(row, PER)
    block_col = floor_div(col, PER)
    rank = along((block_row == block_col) & (col < row) & (number > 0.0), jnp.ones_like(number))
    name = rank + LIVE * block_row[:, :1].astype(jnp.float32)
    position = jnp.sum(
        jnp.where(slot_column == col.astype(jnp.float32), row.astype(jnp.float32), 0.0), axis=0, keepdims=True
    )
    held = (position >= ends - own) & (position < ends)
    item = jnp.sum(jnp.where(held, name, 0.0), axis=0, keepdims=True)
    item_ref[...] = item.astype(jnp.int32)
    devices = total // PER
    to = lax.broadcasted_iota(jnp.int32, (devices, total), 0)
    s = lax.broadcasted_iota(jnp.int32, (devices, total), 1)
    lane = lax.broadcasted_iota(jnp.int32, (devices, 128), 1)
    wide = jnp.full((devices, 128), -1.0, jnp.float32)
    items = jnp.broadcast_to(item, (devices, total))
    for q in range(PER):
        column = jnp.sum(jnp.where(s == to * PER + q, items, 0.0), axis=1, keepdims=True)
        wide = jnp.where((lane >= NBINS * q) & (lane < NBINS * (q + 1)), column, wide)
    wide_ref[...] = wide.astype(jnp.int32)
    lane = lax.broadcasted_iota(jnp.int32, (L, 128), 1)
    for pair in range(2):
        halves = []
        for odd in range(2):
            bins = bins_ref[2 * pair + odd]
            halves.append(jnp.where(lane <= L // 2, bins, pltpu.roll(bins, L // 2, axis=1)))
        map_ref[pair * L : (pair + 1) * L, :] = jnp.where(lane < L, halves[0], pltpu.roll(halves[1], L, axis=1))


def beside(v, lane):
    swapped = pltpu.roll(v, L, axis=1)
    rows = v.shape[0]
    y = swapped + jnp.where(lane < L, pltpu.roll(swapped, 1, axis=0), pltpu.roll(swapped, rows - 1, axis=0))
    inner = lane & (L - 1)
    low = pltpu.roll(jnp.where(inner == L - 1, swapped, v), 1, axis=1)
    high = pltpu.roll(jnp.where(inner == 0, swapped, v), 127, axis=1)
    return y + (low + high)


def sweep_kernel(
    base_ref, counts_ref, field, noise, masses, lo, hi, along_x, along_y, pieces, chunks, fbuf, nbuf, mbuf, sems
):
    live = live_of(counts_ref, base_ref[0])
    first = pltpu.make_async_copy(masses, mbuf, sems.at[3 * LIVE])
    first.start()
    copies = []
    for k in range(LIVE):
        copies.append(
            [
                pltpu.make_async_copy(field.at[live[k]], fbuf.at[k], sems.at[3 * k]),
                pltpu.make_async_copy(noise.at[0, live[k]], nbuf.at[0, k], sems.at[3 * k + 1]),
                pltpu.make_async_copy(noise.at[1, live[k]], nbuf.at[1, k], sems.at[3 * k + 2]),
            ]
        )
        for copy in copies[-1]:
            copy.start()
    first.wait()
    lane = lax.broadcasted_iota(jnp.int32, (ROWS, 128), 1)
    kick = float(np.sqrt(np.float32(0.2)))

    def update(center, below, above, mass, noise_now):
        near = below + above + beside(center, lane)
        return center * (0.4 - 0.1 * mass - 0.05 * (center * center)) + 0.1 * near + kick * noise_now

    def planes(ref, *at):
        return [ref[(*at, pl.ds(z, ROWS, stride=DEPTH), slice(None))] for z in range(DEPTH)]

    mass = [lo[3 * LIVE]] + planes(mbuf) + [hi[3 * LIVE]]
    left = []
    for k in range(LIVE):
        for copy in copies[k]:
            copy.wait()
        old = [lo[2 * k], lo[2 * k + 1]] + planes(fbuf, k) + [hi[2 * k], hi[2 * k + 1]]
        kicks = [lo[2 * LIVE + k]] + planes(nbuf, 0, k) + [hi[2 * LIVE + k]]
        mid = [update(old[p + 1], old[p], old[p + 2], mass[p], kicks[p]) for p in range(DEPTH + 2)]
        kicks = planes(nbuf, 1, k)
        new = [update(mid[p + 1], mid[p], mid[p + 2], mass[p + 1], kicks[p]) for p in range(DEPTH)]
        for z in range(DEPTH):
            pieces[pl.ds(k * DEPTH + z, ROWS, stride=LIVE * DEPTH), :] = new[z]
        left += [jnp.concatenate(new[0:2], axis=1), jnp.concatenate(new[2:4], axis=1)]
    high, low = split(jnp.concatenate(left, axis=0))
    across = dot(high, along_x[0]) + (dot(low, along_x[0]) + dot(high, along_x[1]))
    parts = [across[i * ROWS : (i + 1) * ROWS] for i in range(2 * LIVE)]
    right = jnp.concatenate([jnp.concatenate([p[:, :128], p[:, 128:]], axis=0) for p in parts], axis=1)
    high, low = split(right)
    turned = dot(along_y[0], high) + (dot(along_y[0], low) + dot(along_y[1], high))
    for i in range(2 * LIVE):
        even = turned[:ROWS, 128 * i : 128 * (i + 1)]
        odd = turned[ROWS:, 128 * i : 128 * (i + 1)]
        ready = (
            jnp.where(lane < L, even, pltpu.roll(odd, L, axis=1)),
            jnp.where(lane < L, pltpu.roll(even, L, axis=1), odd),
        )
        for side in range(2):
            for pair in range(2):
                chunks[pl.ds(i * 4 + side * 2 + pair, 16, stride=8 * LIVE), :] = ready[side][16 * pair : 16 * pair + 16]


def bins_kernel(chunks, map_ref, along_z, out, rows):
    place = map_ref[...]
    power = []
    for k in range(LIVE):
        high, low = split(chunks[:, 8 * k : 8 * k + 8, :].reshape(128, 128))
        mode = dot(along_z[0], high) + (dot(along_z[0], low) + dot(along_z[1], high))
        power.append(mode * mode)
    power.append(jnp.ones_like(power[0]))
    for b in range(NBINS):
        here = place == b
        for k in range(LIVE + 1):
            rows[k * NBINS + b : k * NBINS + b + 1, :] = jnp.sum(
                jnp.where(here, power[k], 0.0), axis=0, keepdims=True
            )
    rows[(LIVE + 1) * NBINS :, :] = jnp.zeros((128 - (LIVE + 1) * NBINS, 128), jnp.float32)
    sums = lax.dot_general(
        jnp.ones((8, 128), jnp.float32),
        rows[...],
        (((1,), (1,)), ((), ())),
        precision=lax.Precision.HIGHEST,
        preferred_element_type=jnp.float32,
    )
    out[...] = sums[0:1]


def pick_kernel(item_ref, me_ref, pieces, sums, wide, out):
    total = item_ref.shape[0]
    devices = total // PER
    lane = lax.broadcasted_iota(jnp.int32, (1, 128), 1)
    summed = sums[...]

    def spread(k):
        v = jnp.where((lane >= NBINS * k) & (lane < NBINS * (k + 1)), summed, 0.0)
        for shift in (16, 32, 64):
            v = v + pltpu.roll(v, shift, axis=1)
        return v

    weight = spread(LIVE)
    mine = jnp.zeros((devices, 128), jnp.float32)
    for k in range(LIVE):
        mine = jnp.where(wide[...] == me_ref[0] * LIVE + k, spread(k) / weight, mine)
    for d in range(devices):
        for q in range(PER):
            out[d * (PER + 1) + q] = pieces[item_ref[d * PER + q]]
        out[d * (PER + 1) + PER] = jnp.broadcast_to(mine[d : d + 1], (DEPTH, 128))


def finish_kernel(got, resampled, propagator):
    devices = got.shape[0] // (PER + 1)
    sums = got[PER]
    for d in range(1, devices):
        sums = sums + got[d * (PER + 1) + PER]
    for q in range(PER):
        for d in range(devices):
            resampled[q, :, 128 * d : 128 * (d + 1)] = got[d * (PER + 1) + q]
    for q in range(PER):
        turned = sums if q == 0 else pltpu.roll(sums, 128 - NBINS * q, axis=1)
        propagator[q : q + 1, :] = turned[0:1, :NBINS]


def spec(space):
    return pl.BlockSpec(memory_space=space)


def shape(*dims, dtype=jnp.float32):
    return jax.ShapeDtypeStruct(dims, dtype)


def rows_view(slabs):
    lead = slabs.shape[:-2]
    parts = slabs.reshape(*lead, DEPTH, ROWS, 128)
    return jnp.swapaxes(parts, -3, -2).reshape(*lead, DEPTH * ROWS, 128)


def edges(base, counts, field, noise, masses):
    return pl.pallas_call(
        edges_kernel,
        out_shape=[shape(3 * LIVE + 1, ROWS, 128)] * 2,
        in_specs=[spec(SMEM)] * 2 + [spec(pl.ANY)] * 3,
        out_specs=[spec(VMEM)] * 2,
        scratch_shapes=[
            VMEM((LIVE, 128, 128), jnp.float32),
            VMEM((LIVE, 128, 128), jnp.float32),
            VMEM((128, 128), jnp.float32),
            pltpu.SemaphoreType.DMA((2 * LIVE + 1,)),
        ],
        name="edges",
    )(base, counts, field, noise, masses)


def plan(counts, dest_slots, mode_bins):
    total = counts.shape[0]
    padded = jnp.pad(mode_bins, ((0, 0), (0, 0), (0, 128 - mode_bins.shape[2])))
    return pl.pallas_call(
        plan_kernel,
        out_shape=[
            shape(1, total, dtype=jnp.int32),
            shape(total // PER, 128, dtype=jnp.int32),
            shape(128, 128, dtype=jnp.int32),
        ],
        in_specs=[spec(VMEM)] * 3,
        out_specs=[spec(VMEM)] * 3,
        name="plan",
    )(counts.reshape(1, total), dest_slots.reshape(1, total), padded)


def sweeps(base, counts, field, noise, masses, lo, hi, along_x, along_y):
    return pl.pallas_call(
        sweep_kernel,
        out_shape=[shape(ROWS * LIVE * DEPTH, 128), shape(16 * 8 * LIVE, 128)],
        in_specs=[spec(SMEM)] * 2 + [spec(pl.ANY)] * 3 + [spec(VMEM)] * 4,
        out_specs=[spec(VMEM)] * 2,
        scratch_shapes=[
            VMEM((LIVE, 128, 128), jnp.float32),
            VMEM((2, LIVE, 128, 128), jnp.float32),
            VMEM((128, 128), jnp.float32),
            pltpu.SemaphoreType.DMA((3 * LIVE + 1,)),
        ],
        name="sweeps",
    )(base, counts, field, noise, masses, lo, hi, along_x, along_y)


def bins(chunks, place, along_z):
    return pl.pallas_call(
        bins_kernel,
        out_shape=shape(1, 128),
        in_specs=[spec(VMEM)] * 3,
        out_specs=spec(VMEM),
        scratch_shapes=[VMEM((128, 128), jnp.float32)],
        name="bins",
    )(chunks, place, along_z)


def pick(item, me, pieces, sums, wide):
    devices = item.shape[0] // PER
    return pl.pallas_call(
        pick_kernel,
        out_shape=shape(devices * (PER + 1), DEPTH, 128),
        in_specs=[spec(SMEM)] * 2 + [spec(VMEM)] * 3,
        out_specs=spec(VMEM),
        name="pick",
    )(item, me, pieces, sums, wide)


def finish(got):
    return pl.pallas_call(
        finish_kernel,
        out_shape=[shape(PER, DEPTH, L * L), shape(PER, NBINS)],
        in_specs=[spec(VMEM)],
        out_specs=[spec(VMEM)] * 2,
        name="finish",
    )(got)


def local(lattice_field, langevin_noise, masses, counts, dest_slots, mode_bins):
    along_x, along_y, along_z = (jnp.asarray(t) for t in tables())
    me = lax.axis_index("rep").astype(jnp.int32).reshape(1)
    base = me * PER
    field, noise, mass = rows_view(lattice_field), rows_view(langevin_noise), rows_view(masses)
    up, down = edges(base, counts, field, noise, mass)
    ring = lax.axis_size("gz")
    forward = [(i, (i + 1) % ring) for i in range(ring)]
    lo = lax.ppermute(up, "gz", forward)
    hi = lax.ppermute(down, "gz", [(b, a) for a, b in forward])
    lo, hi, item, wide, place = lax.optimization_barrier((lo, hi, *plan(counts, dest_slots, mode_bins)))
    pieces, chunks = sweeps(base, counts, field, noise, mass, lo, hi, along_x, along_y)
    reps = lax.axis_size("rep")
    chunks = lax.all_to_all(chunks.reshape(ring, 8 * LIVE, 128), "gz", 0, 0, tiled=True)
    pieces, sums = lax.optimization_barrier((pieces, bins(chunks, place, along_z)))
    pieces = lax.all_to_all(pieces.reshape(reps, LIVE, DEPTH, 128), "rep", 0, 0, tiled=True)
    step = 1
    while step < ring:
        sums = sums + lax.ppermute(sums, "gz", [(i, i ^ step) for i in range(ring)])
        step *= 2
    out = pick(item.reshape(-1), me, pieces.reshape(reps * LIVE, DEPTH, 128), sums, wide)
    got = lax.all_to_all(out.reshape(reps, PER + 1, DEPTH, 128), "rep", 0, 0, tiled=True)
    resampled, propagator = finish(got.reshape(reps * (PER + 1), DEPTH, 128))
    return resampled, propagator


def solution(mesh):
    in_specs = (
        P("rep", "gz", None),
        P(None, "rep", "gz", None),
        P("gz", None),
        P(),
        P(),
        P("gz", None, None),
    )
    out_specs = (P("rep", "gz", None), P("rep", None))
    return jax.shard_map(local, mesh=mesh, in_specs=in_specs, out_specs=out_specs, check_vma=False)
```

```python
import jax
import jax.numpy as jnp
import ml_dtypes
import numpy as np
from jax import lax
from jax.experimental import pallas as pl
from jax.experimental.pallas import tpu as pltpu
from jax.sharding import PartitionSpec as P

L = 64
NBINS = 16
LIVE = 3
DEPTH = 4
ROWS = 32
PER = 6
BLOCKS = LIVE + 1

VMEM = pltpu.VMEM
SMEM = pltpu.SMEM


def split_constant(table):
    table = table.astype(np.float32)
    high = table.astype(ml_dtypes.bfloat16)
    low = (table - high.astype(np.float32)).astype(ml_dtypes.bfloat16)
    return np.stack([high, low])


def real_basis(sine_wave):
    slot = np.arange(L)[:, None]
    site = np.arange(L)[None, :]
    wave = np.where(slot <= L // 2, slot, sine_wave(slot))
    angle = 2.0 * np.pi / L * (wave * site % L)
    basis = np.where(slot <= L // 2, np.cos(angle), np.sin(angle)) * np.sqrt(2.0)
    basis[0] = 1.0
    basis[L // 2] = np.cos(np.pi * np.arange(L))
    return basis / np.sqrt(L)


def tables():
    basis_x = real_basis(lambda slot: slot - L // 2)
    basis_k = real_basis(lambda slot: L - slot)
    along_x = np.einsum("ab,cd,mx->acxdbm", np.eye(2), np.eye(2), basis_x).reshape(256, 256)
    along_y = basis_k.reshape(16, 2, 2, 32, 2).transpose(2, 1, 0, 4, 3).reshape(64, 64)
    along_z = np.einsum("ab,kz->akzb", np.eye(2), basis_k).reshape(128, 128)
    return split_constant(along_x), split_constant(along_y), split_constant(along_z)


def split(value):
    high = value.astype(jnp.bfloat16)
    return high, (value - high.astype(jnp.float32)).astype(jnp.bfloat16)


def dot(a, b):
    return jnp.dot(a, b, preferred_element_type=jnp.float32)


def live_of(counts_ref, base):
    seen = jnp.int32(0)
    live = [jnp.int32(0)] * LIVE
    for j in range(PER):
        alive = counts_ref[base + j] > 0
        for k in range(LIVE):
            live[k] = jnp.where(alive & (seen == k), j, live[k])
        seen = seen + alive.astype(jnp.int32)
    return live


def edges_kernel(base_ref, counts_ref, field, noise, masses, up, down, fbuf, nbuf, mbuf, sems):
    live = live_of(counts_ref, base_ref[0])
    copies = [pltpu.make_async_copy(masses, mbuf, sems.at[2 * LIVE])]
    for k in range(LIVE):
        copies.append(pltpu.make_async_copy(field.at[live[k]], fbuf.at[k], sems.at[2 * k]))
        copies.append(pltpu.make_async_copy(noise.at[0, live[k]], nbuf.at[k], sems.at[2 * k + 1]))
    for copy in copies:
        copy.start()
    for copy in copies:
        copy.wait()
    for k in range(LIVE):
        up[2 * k] = fbuf[k, pl.ds(2, ROWS, stride=DEPTH), :]
        up[2 * k + 1] = fbuf[k, pl.ds(3, ROWS, stride=DEPTH), :]
        down[2 * k] = fbuf[k, pl.ds(0, ROWS, stride=DEPTH), :]
        down[2 * k + 1] = fbuf[k, pl.ds(1, ROWS, stride=DEPTH), :]
        up[2 * LIVE + k] = nbuf[k, pl.ds(3, ROWS, stride=DEPTH), :]
        down[2 * LIVE + k] = nbuf[k, pl.ds(0, ROWS, stride=DEPTH), :]
    up[3 * LIVE] = mbuf[pl.ds(3, ROWS, stride=DEPTH), :]
    down[3 * LIVE] = mbuf[pl.ds(0, ROWS, stride=DEPTH), :]


def floor_div(value, by):
    return jnp.floor((value.astype(jnp.float32) + 0.5) * (1.0 / by)).astype(jnp.int32)


def plan_kernel(counts_ref, slots_ref, bins_ref, item_ref, wide_ref, map_ref):
    total = counts_ref.shape[1]
    row = lax.broadcasted_iota(jnp.int32, (total, total), 0)
    col = lax.broadcasted_iota(jnp.int32, (total, total), 1)
    number = jnp.broadcast_to(counts_ref[...].astype(jnp.float32), (total, total))
    slot = jnp.broadcast_to(slots_ref[...].astype(jnp.float32), (total, total))

    def along(mask, value):
        return jnp.sum(jnp.where(mask, value, 0.0), axis=1, keepdims=True)

    own = along(row == col, number)
    ends = along(col <= row, number)
    slot_column = along(row == col, slot)
    block_row = floor_div(row, PER)
    block_col = floor_div(col, PER)
    rank = along((block_row == block_col) & (col < row) & (number > 0.0), jnp.ones_like(number))
    name = rank + BLOCKS * block_row[:, :1].astype(jnp.float32)
    position = jnp.sum(
        jnp.where(slot_column == col.astype(jnp.float32), row.astype(jnp.float32), 0.0), axis=0, keepdims=True
    )
    held = (position >= ends - own) & (position < ends)
    item = jnp.sum(jnp.where(held, name, 0.0), axis=0, keepdims=True)
    item_ref[...] = item.astype(jnp.int32)
    devices = total // PER
    to = lax.broadcasted_iota(jnp.int32, (devices, total), 0)
    s = lax.broadcasted_iota(jnp.int32, (devices, total), 1)
    lane = lax.broadcasted_iota(jnp.int32, (devices, 128), 1)
    wide = jnp.full((devices, 128), -1.0, jnp.float32)
    items = jnp.broadcast_to(item, (devices, total))
    for q in range(PER):
        column = jnp.sum(jnp.where(s == to * PER + q, items, 0.0), axis=1, keepdims=True)
        wide = jnp.where((lane >= NBINS * q) & (lane < NBINS * (q + 1)), column, wide)
    wide_ref[...] = wide.astype(jnp.int32)
    lane = lax.broadcasted_iota(jnp.int32, (L, 128), 1)
    for pair in range(2):
        halves = []
        for odd in range(2):
            bins = bins_ref[2 * pair + odd]
            halves.append(jnp.where(lane <= L // 2, bins, pltpu.roll(bins, L // 2, axis=1)))
        map_ref[pair * L : (pair + 1) * L, :] = jnp.where(lane < L, halves[0], pltpu.roll(halves[1], L, axis=1))


def beside(v, lane):
    swapped = pltpu.roll(v, L, axis=1)
    rows = v.shape[0]
    y = swapped + jnp.where(lane < L, pltpu.roll(swapped, 1, axis=0), pltpu.roll(swapped, rows - 1, axis=0))
    inner = lane & (L - 1)
    low = pltpu.roll(jnp.where(inner == L - 1, swapped, v), 1, axis=1)
    high = pltpu.roll(jnp.where(inner == 0, swapped, v), 127, axis=1)
    return y + (low + high)


def sweep_kernel(
    base_ref, counts_ref, field, noise, masses, lo, hi, along_x, along_y, pieces, chunks, fbuf, nbuf, mbuf, sems
):
    live = live_of(counts_ref, base_ref[0])
    first = pltpu.make_async_copy(masses, mbuf, sems.at[3 * LIVE])
    first.start()
    copies = []
    for k in range(LIVE):
        copies.append(
            [
                pltpu.make_async_copy(field.at[live[k]], fbuf.at[k], sems.at[3 * k]),
                pltpu.make_async_copy(noise.at[0, live[k]], nbuf.at[0, k], sems.at[3 * k + 1]),
                pltpu.make_async_copy(noise.at[1, live[k]], nbuf.at[1, k], sems.at[3 * k + 2]),
            ]
        )
        for copy in copies[-1]:
            copy.start()
    first.wait()
    lane = lax.broadcasted_iota(jnp.int32, (ROWS, 128), 1)
    kick = float(np.sqrt(np.float32(0.2)))

    def update(center, below, above, mass, noise_now):
        near = below + above + beside(center, lane)
        return center * (0.4 - 0.1 * mass - 0.05 * (center * center)) + 0.1 * near + kick * noise_now

    def planes(ref, *at):
        return [ref[(*at, pl.ds(z, ROWS, stride=DEPTH), slice(None))] for z in range(DEPTH)]

    mass = [lo[3 * LIVE]] + planes(mbuf) + [hi[3 * LIVE]]
    left = []
    for k in range(LIVE):
        for copy in copies[k]:
            copy.wait()
        old = [lo[2 * k], lo[2 * k + 1]] + planes(fbuf, k) + [hi[2 * k], hi[2 * k + 1]]
        kicks = [lo[2 * LIVE + k]] + planes(nbuf, 0, k) + [hi[2 * LIVE + k]]
        mid = [update(old[p + 1], old[p], old[p + 2], mass[p], kicks[p]) for p in range(DEPTH + 2)]
        kicks = planes(nbuf, 1, k)
        new = [update(mid[p + 1], mid[p], mid[p + 2], mass[p + 1], kicks[p]) for p in range(DEPTH)]
        for z in range(DEPTH):
            pieces[pl.ds(k * DEPTH + z, ROWS, stride=BLOCKS * DEPTH), :] = new[z]
        left += [jnp.concatenate(new[0:2], axis=1), jnp.concatenate(new[2:4], axis=1)]
    high, low = split(jnp.concatenate(left, axis=0))
    across = dot(high, along_x[0]) + (dot(low, along_x[0]) + dot(high, along_x[1]))
    parts = [across[i * ROWS : (i + 1) * ROWS] for i in range(2 * LIVE)]
    right = jnp.concatenate([jnp.concatenate([p[:, :128], p[:, 128:]], axis=0) for p in parts], axis=1)
    high, low = split(right)
    turned = dot(along_y[0], high) + (dot(along_y[0], low) + dot(along_y[1], high))
    for i in range(2 * LIVE):
        even = turned[:ROWS, 128 * i : 128 * (i + 1)]
        odd = turned[ROWS:, 128 * i : 128 * (i + 1)]
        ready = (
            jnp.where(lane < L, even, pltpu.roll(odd, L, axis=1)),
            jnp.where(lane < L, pltpu.roll(even, L, axis=1), odd),
        )
        for side in range(2):
            for pair in range(2):
                chunks[pl.ds(i * 4 + side * 2 + pair, 16, stride=8 * LIVE), :] = ready[side][16 * pair : 16 * pair + 16]


def bins_kernel(me_ref, chunks, map_ref, wide, along_z, _, pieces, rows, block, sem):
    devices = wide.shape[0]
    place = map_ref[...]
    power = []
    for k in range(LIVE):
        high, low = split(chunks[:, 8 * k : 8 * k + 8, :].reshape(128, 128))
        mode = dot(along_z[0], high) + (dot(along_z[0], low) + dot(along_z[1], high))
        power.append(mode * mode)
    power.append(jnp.ones_like(power[0]))
    for b in range(NBINS):
        here = place == b
        for k in range(BLOCKS):
            rows[k * NBINS + b : k * NBINS + b + 1, :] = jnp.sum(
                jnp.where(here, power[k], 0.0), axis=0, keepdims=True
            )
    rows[BLOCKS * NBINS :, :] = jnp.zeros((128 - BLOCKS * NBINS, 128), jnp.float32)
    sums = lax.dot_general(
        jnp.ones((8, 128), jnp.float32),
        rows[...],
        (((1,), (1,)), ((), ())),
        precision=lax.Precision.HIGHEST,
        preferred_element_type=jnp.float32,
    )[0:1]
    lane = lax.broadcasted_iota(jnp.int32, (1, 128), 1)
    mine = jnp.where(lane >= NBINS * PER, spread(sums, LIVE, lane) * (1.0 / devices), 0.0)
    mine = jnp.broadcast_to(mine, (devices, 128))
    for k in range(LIVE):
        mine = jnp.where(wide[...] == me_ref[0] * BLOCKS + k, spread(sums, k, lane), mine)
    for d in range(devices):
        block[d] = jnp.broadcast_to(mine[d : d + 1], (DEPTH, 128))
    copy = pltpu.make_async_copy(block, pieces.at[:, LIVE], sem)
    copy.start()
    copy.wait()


def spread(row, k, lane):
    row = jnp.where((lane >= NBINS * k) & (lane < NBINS * (k + 1)), row, 0.0)
    for shift in (16, 32, 64):
        row = row + pltpu.roll(row, shift, axis=1)
    return row


def pick_kernel(item_ref, pieces, out, part):
    devices = pieces.shape[0] // BLOCKS
    for s in range(devices * PER):
        out[s] = pieces[item_ref[s]]
    sums = pieces[LIVE]
    for d in range(1, devices):
        sums = sums + pieces[d * BLOCKS + LIVE]
    part[...] = sums[0:1]


def finish_kernel(got, sums_ref, resampled, propagator):
    devices = got.shape[0] // PER
    for q in range(PER):
        for d in range(devices):
            resampled[q, :, 128 * d : 128 * (d + 1)] = got[d * PER + q]
    lane = lax.broadcasted_iota(jnp.int32, (1, 128), 1)
    ratio = sums_ref[...] / spread(sums_ref[...], PER, lane)
    for q in range(PER):
        turned = ratio if q == 0 else pltpu.roll(ratio, 128 - NBINS * q, axis=1)
        propagator[q : q + 1, :] = turned[:, :NBINS]


def spec(space):
    return pl.BlockSpec(memory_space=space)


def shape(*dims, dtype=jnp.float32):
    return jax.ShapeDtypeStruct(dims, dtype)


def rows_view(slabs):
    lead = slabs.shape[:-2]
    parts = slabs.reshape(*lead, DEPTH, ROWS, 128)
    return jnp.swapaxes(parts, -3, -2).reshape(*lead, DEPTH * ROWS, 128)


def edges(base, counts, field, noise, masses):
    return pl.pallas_call(
        edges_kernel,
        out_shape=[shape(3 * LIVE + 1, ROWS, 128)] * 2,
        in_specs=[spec(SMEM)] * 2 + [spec(pl.ANY)] * 3,
        out_specs=[spec(VMEM)] * 2,
        scratch_shapes=[
            VMEM((LIVE, 128, 128), jnp.float32),
            VMEM((LIVE, 128, 128), jnp.float32),
            VMEM((128, 128), jnp.float32),
            pltpu.SemaphoreType.DMA((2 * LIVE + 1,)),
        ],
        name="edges",
    )(base, counts, field, noise, masses)


def plan(counts, dest_slots, mode_bins):
    total = counts.shape[0]
    padded = jnp.pad(mode_bins, ((0, 0), (0, 0), (0, 128 - mode_bins.shape[2])))
    return pl.pallas_call(
        plan_kernel,
        out_shape=[
            shape(1, total, dtype=jnp.int32),
            shape(total // PER, 128, dtype=jnp.int32),
            shape(128, 128, dtype=jnp.int32),
        ],
        in_specs=[spec(VMEM)] * 3,
        out_specs=[spec(VMEM)] * 3,
        name="plan",
    )(counts.reshape(1, total), dest_slots.reshape(1, total), padded)


def sweeps(base, counts, field, noise, masses, lo, hi, along_x, along_y):
    return pl.pallas_call(
        sweep_kernel,
        out_shape=[shape(ROWS * BLOCKS * DEPTH, 128), shape(16 * 8 * LIVE, 128)],
        in_specs=[spec(SMEM)] * 2 + [spec(pl.ANY)] * 3 + [spec(VMEM)] * 4,
        out_specs=[spec(VMEM)] * 2,
        scratch_shapes=[
            VMEM((LIVE, 128, 128), jnp.float32),
            VMEM((2, LIVE, 128, 128), jnp.float32),
            VMEM((128, 128), jnp.float32),
            pltpu.SemaphoreType.DMA((3 * LIVE + 1,)),
        ],
        name="sweeps",
    )(base, counts, field, noise, masses, lo, hi, along_x, along_y)


def bins(me, chunks, place, wide, along_z, pieces):
    devices = wide.shape[0]
    return pl.pallas_call(
        bins_kernel,
        out_shape=shape(devices, BLOCKS, DEPTH, 128),
        in_specs=[spec(SMEM)] + [spec(VMEM)] * 4 + [spec(pl.ANY)],
        out_specs=spec(pl.ANY),
        scratch_shapes=[
            VMEM((128, 128), jnp.float32),
            VMEM((devices, DEPTH, 128), jnp.float32),
            pltpu.SemaphoreType.DMA,
        ],
        input_output_aliases={5: 0},
        name="bins",
    )(me, chunks, place, wide, along_z, pieces)


def pick(item, pieces):
    return pl.pallas_call(
        pick_kernel,
        out_shape=[shape(item.shape[0], DEPTH, 128), shape(1, 128)],
        in_specs=[spec(SMEM), spec(VMEM)],
        out_specs=[spec(VMEM)] * 2,
        name="pick",
    )(item, pieces)


def finish(got, sums):
    return pl.pallas_call(
        finish_kernel,
        out_shape=[shape(PER, DEPTH, L * L), shape(PER, NBINS)],
        in_specs=[spec(VMEM)] * 2,
        out_specs=[spec(VMEM)] * 2,
        name="finish",
    )(got, sums)


def local(lattice_field, langevin_noise, masses, counts, dest_slots, mode_bins):
    along_x, along_y, along_z = (jnp.asarray(t) for t in tables())
    me = lax.axis_index("rep").astype(jnp.int32).reshape(1)
    base = me * PER
    field, noise, mass = rows_view(lattice_field), rows_view(langevin_noise), rows_view(masses)
    up, down = edges(base, counts, field, noise, mass)
    ring = lax.axis_size("gz")
    forward = [(i, (i + 1) % ring) for i in range(ring)]
    lo = lax.ppermute(up, "gz", forward)
    hi = lax.ppermute(down, "gz", [(b, a) for a, b in forward])
    lo, hi, item, wide, place = lax.optimization_barrier((lo, hi, *plan(counts, dest_slots, mode_bins)))
    pieces, chunks = sweeps(base, counts, field, noise, mass, lo, hi, along_x, along_y)
    reps = lax.axis_size("rep")
    chunks = lax.all_to_all(chunks.reshape(ring, 8 * LIVE, 128), "gz", 0, 0, tiled=True)
    pieces = bins(me, chunks, place, wide, along_z, pieces.reshape(reps, BLOCKS, DEPTH, 128))
    pieces = lax.all_to_all(pieces, "rep", 0, 0, tiled=True)
    out, sums = pick(item.reshape(-1), pieces.reshape(reps * BLOCKS, DEPTH, 128))
    got = lax.all_to_all(out.reshape(reps, PER, DEPTH, 128), "rep", 0, 0, tiled=True)
    step = 1
    while step < ring:
        sums = sums + lax.ppermute(sums, "gz", [(i, i ^ step) for i in range(ring)])
        step *= 2
    resampled, propagator = finish(got.reshape(reps * PER, DEPTH, 128), sums)
    return resampled, propagator


def solution(mesh):
    in_specs = (
        P("rep", "gz", None),
        P(None, "rep", "gz", None),
        P("gz", None),
        P(),
        P(),
        P("gz", None, None),
    )
    out_specs = (P("rep", "gz", None), P("rep", None))
    return jax.shard_map(local, mesh=mesh, in_specs=in_specs, out_specs=out_specs, check_vma=False)
```

```python
import jax
import jax.numpy as jnp
import ml_dtypes
import numpy as np
from jax import lax
from jax.experimental import pallas as pl
from jax.experimental.pallas import tpu as pltpu
from jax.sharding import PartitionSpec as P

L = 64
NBINS = 16
LIVE = 3
DEPTH = 4
ROWS = 32
PER = 6
BLOCKS = LIVE + 1

VMEM = pltpu.VMEM
SMEM = pltpu.SMEM


def split_constant(table):
    table = table.astype(np.float32)
    high = table.astype(ml_dtypes.bfloat16)
    low = (table - high.astype(np.float32)).astype(ml_dtypes.bfloat16)
    return np.stack([high, low])


def real_basis(sine_wave):
    slot = np.arange(L)[:, None]
    site = np.arange(L)[None, :]
    wave = np.where(slot <= L // 2, slot, sine_wave(slot))
    angle = 2.0 * np.pi / L * (wave * site % L)
    basis = np.where(slot <= L // 2, np.cos(angle), np.sin(angle)) * np.sqrt(2.0)
    basis[0] = 1.0
    basis[L // 2] = np.cos(np.pi * np.arange(L))
    return basis / np.sqrt(L)


def tables():
    basis_x = real_basis(lambda slot: slot - L // 2)
    basis_k = real_basis(lambda slot: L - slot)
    along_x = np.einsum("ab,cd,mx->acxdbm", np.eye(2), np.eye(2), basis_x).reshape(256, 256)
    along_y = basis_k.reshape(16, 2, 2, 32, 2).transpose(2, 1, 0, 4, 3).reshape(64, 64)
    along_z = np.einsum("ab,kz->akzb", np.eye(2), basis_k).reshape(128, 128)
    return split_constant(along_x), split_constant(along_y), split_constant(along_z)


def split(value):
    high = value.astype(jnp.bfloat16)
    return high, (value - high.astype(jnp.float32)).astype(jnp.bfloat16)


def dot(a, b):
    return jnp.dot(a, b, preferred_element_type=jnp.float32)


def live_of(counts_ref, base):
    seen = jnp.int32(0)
    live = [jnp.int32(0)] * LIVE
    for j in range(PER):
        alive = counts_ref[base + j] > 0
        for k in range(LIVE):
            live[k] = jnp.where(alive & (seen == k), j, live[k])
        seen = seen + alive.astype(jnp.int32)
    return live


def planes(ref, *at):
    return [ref[(*at, pl.ds(z, ROWS, stride=DEPTH), slice(None))] for z in range(DEPTH)]


def beside(v, lane):
    swapped = pltpu.roll(v, L, axis=1)
    rows = v.shape[0]
    y = swapped + jnp.where(lane < L, pltpu.roll(swapped, 1, axis=0), pltpu.roll(swapped, rows - 1, axis=0))
    inner = lane & (L - 1)
    low = pltpu.roll(jnp.where(inner == L - 1, swapped, v), 1, axis=1)
    high = pltpu.roll(jnp.where(inner == 0, swapped, v), 127, axis=1)
    return y + (low + high)


KICK = float(np.sqrt(np.float32(0.2)))


def update(center, near, mass, noise_now, lane):
    near = near + beside(center, lane)
    return center * (0.4 - 0.1 * mass - 0.05 * (center * center)) + 0.1 * near + KICK * noise_now


def edges_kernel(base_ref, counts_ref, field, noise, masses, up, down, mid, fbuf, nbuf, mbuf, sems):
    live = live_of(counts_ref, base_ref[0])
    first = pltpu.make_async_copy(masses, mbuf, sems.at[2 * LIVE])
    first.start()
    copies = []
    for k in range(LIVE):
        copies.append(
            [
                pltpu.make_async_copy(field.at[live[k]], fbuf.at[k], sems.at[2 * k]),
                pltpu.make_async_copy(noise.at[0, live[k]], nbuf.at[k], sems.at[2 * k + 1]),
            ]
        )
        for copy in copies[-1]:
            copy.start()
    first.wait()
    lane = lax.broadcasted_iota(jnp.int32, (ROWS, 128), 1)
    mass = planes(mbuf)
    for k in range(LIVE):
        for copy in copies[k]:
            copy.wait()
        old = planes(fbuf, k)
        kicks = planes(nbuf, k)
        near = (old[1], old[0] + old[2], old[1] + old[3], old[2])
        new = [update(old[z], near[z], mass[z], kicks[z], lane) for z in range(DEPTH)]
        down[2 * k] = old[0]
        down[2 * k + 1] = new[0]
        up[2 * k] = old[3]
        up[2 * k + 1] = new[3]
        mid[2 * k] = new[1]
        mid[2 * k + 1] = new[2]


def floor_div(value, by):
    return jnp.floor((value.astype(jnp.float32) + 0.5) * (1.0 / by)).astype(jnp.int32)


def plan_kernel(counts_ref, slots_ref, bins_ref, item_ref, wide_ref, map_ref):
    total = counts_ref.shape[1]
    row = lax.broadcasted_iota(jnp.int32, (total, total), 0)
    col = lax.broadcasted_iota(jnp.int32, (total, total), 1)
    number = jnp.broadcast_to(counts_ref[...].astype(jnp.float32), (total, total))
    slot = jnp.broadcast_to(slots_ref[...].astype(jnp.float32), (total, total))

    def along(mask, value):
        return jnp.sum(jnp.where(mask, value, 0.0), axis=1, keepdims=True)

    own = along(row == col, number)
    ends = along(col <= row, number)
    slot_column = along(row == col, slot)
    block_row = floor_div(row, PER)
    block_col = floor_div(col, PER)
    rank = along((block_row == block_col) & (col < row) & (number > 0.0), jnp.ones_like(number))
    name = rank + BLOCKS * block_row[:, :1].astype(jnp.float32)
    position = jnp.sum(
        jnp.where(slot_column == col.astype(jnp.float32), row.astype(jnp.float32), 0.0), axis=0, keepdims=True
    )
    held = (position >= ends - own) & (position < ends)
    item = jnp.sum(jnp.where(held, name, 0.0), axis=0, keepdims=True)
    item_ref[...] = item.astype(jnp.int32)
    devices = total // PER
    to = lax.broadcasted_iota(jnp.int32, (devices, total), 0)
    s = lax.broadcasted_iota(jnp.int32, (devices, total), 1)
    lane = lax.broadcasted_iota(jnp.int32, (devices, 128), 1)
    wide = jnp.full((devices, 128), -1.0, jnp.float32)
    items = jnp.broadcast_to(item, (devices, total))
    for q in range(PER):
        column = jnp.sum(jnp.where(s == to * PER + q, items, 0.0), axis=1, keepdims=True)
        wide = jnp.where((lane >= NBINS * q) & (lane < NBINS * (q + 1)), column, wide)
    wide_ref[...] = wide.astype(jnp.int32)
    lane = lax.broadcasted_iota(jnp.int32, (L, 128), 1)
    for pair in range(2):
        halves = []
        for odd in range(2):
            bins = bins_ref[2 * pair + odd]
            halves.append(jnp.where(lane <= L // 2, bins, pltpu.roll(bins, L // 2, axis=1)))
        map_ref[pair * L : (pair + 1) * L, :] = jnp.where(lane < L, halves[0], pltpu.roll(halves[1], L, axis=1))


def sweep_kernel(
    base_ref, counts_ref, noise, masses, lo, hi, up, down, mid, along_x, along_y, pieces, chunks, nbuf, mbuf, sems
):
    live = live_of(counts_ref, base_ref[0])
    first = pltpu.make_async_copy(masses, mbuf, sems.at[LIVE])
    first.start()
    copies = [pltpu.make_async_copy(noise.at[1, live[k]], nbuf.at[k], sems.at[k]) for k in range(LIVE)]
    for copy in copies:
        copy.start()
    first.wait()
    lane = lax.broadcasted_iota(jnp.int32, (ROWS, 128), 1)
    mass = planes(mbuf)
    left = []
    for k in range(LIVE):
        copies[k].wait()
        now = [
            lo[2 * k + 1] + 0.1 * down[2 * k],
            down[2 * k + 1] + 0.1 * lo[2 * k],
            mid[2 * k],
            mid[2 * k + 1],
            up[2 * k + 1] + 0.1 * hi[2 * k],
            hi[2 * k + 1] + 0.1 * up[2 * k],
        ]
        kicks = planes(nbuf, k)
        new = [update(now[p + 1], now[p] + now[p + 2], mass[p], kicks[p], lane) for p in range(DEPTH)]
        for z in range(DEPTH):
            pieces[pl.ds(k * DEPTH + z, ROWS, stride=BLOCKS * DEPTH), :] = new[z]
        left += [jnp.concatenate(new[0:2], axis=1), jnp.concatenate(new[2:4], axis=1)]
    high, low = split(jnp.concatenate(left, axis=0))
    across = dot(high, along_x[0]) + (dot(low, along_x[0]) + dot(high, along_x[1]))
    parts = [across[i * ROWS : (i + 1) * ROWS] for i in range(2 * LIVE)]
    right = jnp.concatenate([jnp.concatenate([p[:, :128], p[:, 128:]], axis=0) for p in parts], axis=1)
    high, low = split(right)
    turned = dot(along_y[0], high) + (dot(along_y[0], low) + dot(along_y[1], high))
    for i in range(2 * LIVE):
        even = turned[:ROWS, 128 * i : 128 * (i + 1)]
        odd = turned[ROWS:, 128 * i : 128 * (i + 1)]
        ready = (
            jnp.where(lane < L, even, pltpu.roll(odd, L, axis=1)),
            jnp.where(lane < L, pltpu.roll(even, L, axis=1), odd),
        )
        for side in range(2):
            for pair in range(2):
                chunks[pl.ds(i * 4 + side * 2 + pair, 16, stride=8 * LIVE), :] = ready[side][16 * pair : 16 * pair + 16]


def bins_kernel(me_ref, chunks, map_ref, wide, along_z, _, pieces, rows, block, sem):
    devices = wide.shape[0]
    place = map_ref[...]
    power = []
    for k in range(LIVE):
        high, low = split(chunks[:, 8 * k : 8 * k + 8, :].reshape(128, 128))
        mode = dot(along_z[0], high) + (dot(along_z[0], low) + dot(along_z[1], high))
        power.append(mode * mode)
    power.append(jnp.ones_like(power[0]))
    for b in range(NBINS):
        here = place == b
        for k in range(BLOCKS):
            rows[k * NBINS + b : k * NBINS + b + 1, :] = jnp.sum(
                jnp.where(here, power[k], 0.0), axis=0, keepdims=True
            )
    rows[BLOCKS * NBINS :, :] = jnp.zeros((128 - BLOCKS * NBINS, 128), jnp.float32)
    sums = lax.dot_general(
        jnp.ones((8, 128), jnp.float32),
        rows[...],
        (((1,), (1,)), ((), ())),
        precision=lax.Precision.HIGHEST,
        preferred_element_type=jnp.float32,
    )[0:1]
    lane = lax.broadcasted_iota(jnp.int32, (1, 128), 1)
    mine = jnp.where(lane >= NBINS * PER, spread(sums, LIVE, lane) * (1.0 / devices), 0.0)
    mine = jnp.broadcast_to(mine, (devices, 128))
    for k in range(LIVE):
        mine = jnp.where(wide[...] == me_ref[0] * BLOCKS + k, spread(sums, k, lane), mine)
    for d in range(devices):
        block[d] = jnp.broadcast_to(mine[d : d + 1], (DEPTH, 128))
    copy = pltpu.make_async_copy(block, pieces.at[:, LIVE], sem)
    copy.start()
    copy.wait()


def spread(row, k, lane):
    row = jnp.where((lane >= NBINS * k) & (lane < NBINS * (k + 1)), row, 0.0)
    for shift in (16, 32, 64):
        row = row + pltpu.roll(row, shift, axis=1)
    return row


def pick_kernel(item_ref, pieces, out, part):
    devices = pieces.shape[0] // BLOCKS
    for s in range(devices * PER):
        out[s] = pieces[item_ref[s]]
    sums = pieces[LIVE]
    for d in range(1, devices):
        sums = sums + pieces[d * BLOCKS + LIVE]
    part[...] = sums[0:1]


def finish_kernel(got, sums_ref, resampled, propagator):
    devices = got.shape[0] // PER
    for q in range(PER):
        for d in range(devices):
            resampled[q, :, 128 * d : 128 * (d + 1)] = got[d * PER + q]
    lane = lax.broadcasted_iota(jnp.int32, (1, 128), 1)
    ratio = sums_ref[...] / spread(sums_ref[...], PER, lane)
    for q in range(PER):
        turned = ratio if q == 0 else pltpu.roll(ratio, 128 - NBINS * q, axis=1)
        propagator[q : q + 1, :] = turned[:, :NBINS]


def spec(space):
    return pl.BlockSpec(memory_space=space)


def shape(*dims, dtype=jnp.float32):
    return jax.ShapeDtypeStruct(dims, dtype)


def rows_view(slabs):
    lead = slabs.shape[:-2]
    parts = slabs.reshape(*lead, DEPTH, ROWS, 128)
    return jnp.swapaxes(parts, -3, -2).reshape(*lead, DEPTH * ROWS, 128)


def edges(base, counts, field, noise, masses):
    return pl.pallas_call(
        edges_kernel,
        out_shape=[shape(2 * LIVE, ROWS, 128)] * 3,
        in_specs=[spec(SMEM)] * 2 + [spec(pl.ANY)] * 3,
        out_specs=[spec(VMEM)] * 3,
        scratch_shapes=[
            VMEM((LIVE, 128, 128), jnp.float32),
            VMEM((LIVE, 128, 128), jnp.float32),
            VMEM((128, 128), jnp.float32),
            pltpu.SemaphoreType.DMA((2 * LIVE + 1,)),
        ],
        name="edges",
    )(base, counts, field, noise, masses)


def plan(counts, dest_slots, mode_bins):
    total = counts.shape[0]
    padded = jnp.pad(mode_bins, ((0, 0), (0, 0), (0, 128 - mode_bins.shape[2])))
    return pl.pallas_call(
        plan_kernel,
        out_shape=[
            shape(1, total, dtype=jnp.int32),
            shape(total // PER, 128, dtype=jnp.int32),
            shape(128, 128, dtype=jnp.int32),
        ],
        in_specs=[spec(VMEM)] * 3,
        out_specs=[spec(VMEM)] * 3,
        name="plan",
    )(counts.reshape(1, total), dest_slots.reshape(1, total), padded)


def sweeps(base, counts, noise, masses, *blocks):
    return pl.pallas_call(
        sweep_kernel,
        out_shape=[shape(ROWS * BLOCKS * DEPTH, 128), shape(16 * 8 * LIVE, 128)],
        in_specs=[spec(SMEM)] * 2 + [spec(pl.ANY)] * 2 + [spec(VMEM)] * 7,
        out_specs=[spec(VMEM)] * 2,
        scratch_shapes=[
            VMEM((LIVE, 128, 128), jnp.float32),
            VMEM((128, 128), jnp.float32),
            pltpu.SemaphoreType.DMA((LIVE + 1,)),
        ],
        name="sweeps",
    )(base, counts, noise, masses, *blocks)


def bins(me, chunks, place, wide, along_z, pieces):
    devices = wide.shape[0]
    return pl.pallas_call(
        bins_kernel,
        out_shape=shape(devices, BLOCKS, DEPTH, 128),
        in_specs=[spec(SMEM)] + [spec(VMEM)] * 4 + [spec(pl.ANY)],
        out_specs=spec(pl.ANY),
        scratch_shapes=[
            VMEM((128, 128), jnp.float32),
            VMEM((devices, DEPTH, 128), jnp.float32),
            pltpu.SemaphoreType.DMA,
        ],
        input_output_aliases={5: 0},
        name="bins",
    )(me, chunks, place, wide, along_z, pieces)


def pick(item, pieces):
    return pl.pallas_call(
        pick_kernel,
        out_shape=[shape(item.shape[0], DEPTH, 128), shape(1, 128)],
        in_specs=[spec(SMEM), spec(VMEM)],
        out_specs=[spec(VMEM)] * 2,
        name="pick",
    )(item, pieces)


def finish(got, sums):
    return pl.pallas_call(
        finish_kernel,
        out_shape=[shape(PER, DEPTH, L * L), shape(PER, NBINS)],
        in_specs=[spec(VMEM)] * 2,
        out_specs=[spec(VMEM)] * 2,
        name="finish",
    )(got, sums)


def local(lattice_field, langevin_noise, masses, counts, dest_slots, mode_bins):
    along_x, along_y, along_z = (jnp.asarray(t) for t in tables())
    me = lax.axis_index("rep").astype(jnp.int32).reshape(1)
    base = me * PER
    field, noise, mass = rows_view(lattice_field), rows_view(langevin_noise), rows_view(masses)
    up, down, mid = edges(base, counts, field, noise, mass)
    ring = lax.axis_size("gz")
    forward = [(i, (i + 1) % ring) for i in range(ring)]
    lo = lax.ppermute(up, "gz", forward)
    hi = lax.ppermute(down, "gz", [(b, a) for a, b in forward])
    lo, hi, item, wide, place = lax.optimization_barrier((lo, hi, *plan(counts, dest_slots, mode_bins)))
    pieces, chunks = sweeps(base, counts, noise, mass, lo, hi, up, down, mid, along_x, along_y)
    reps = lax.axis_size("rep")
    chunks = lax.all_to_all(chunks.reshape(ring, 8 * LIVE, 128), "gz", 0, 0, tiled=True)
    pieces = bins(me, chunks, place, wide, along_z, pieces.reshape(reps, BLOCKS, DEPTH, 128))
    pieces = lax.all_to_all(pieces, "rep", 0, 0, tiled=True)
    out, sums = pick(item.reshape(-1), pieces.reshape(reps * BLOCKS, DEPTH, 128))
    got = lax.all_to_all(out.reshape(reps, PER, DEPTH, 128), "rep", 0, 0, tiled=True)
    step = 1
    while step < ring:
        sums = sums + lax.ppermute(sums, "gz", [(i, i ^ step) for i in range(ring)])
        step *= 2
    resampled, propagator = finish(got.reshape(reps * PER, DEPTH, 128), sums)
    return resampled, propagator


def solution(mesh):
    in_specs = (
        P("rep", "gz", None),
        P(None, "rep", "gz", None),
        P("gz", None),
        P(),
        P(),
        P("gz", None, None),
    )
    out_specs = (P("rep", "gz", None), P("rep", None))
    return jax.shard_map(local, mesh=mesh, in_specs=in_specs, out_specs=out_specs, check_vma=False)
```

```python
import jax
import jax.numpy as jnp
import ml_dtypes
import numpy as np
from jax import lax
from jax.experimental import pallas as pl
from jax.experimental.pallas import tpu as pltpu
from jax.sharding import PartitionSpec as P

L = 64
NBINS = 16
LIVE = 3
DEPTH = 4
ROWS = 32
PER = 6
BLOCKS = LIVE + 1
GRANT = 8 << 20

VMEM = pltpu.VMEM
SMEM = pltpu.SMEM


def split_constant(table):
    table = table.astype(np.float32)
    high = table.astype(ml_dtypes.bfloat16)
    low = (table - high.astype(np.float32)).astype(ml_dtypes.bfloat16)
    return np.stack([high, low])


def real_basis(sine_wave):
    slot = np.arange(L)[:, None]
    site = np.arange(L)[None, :]
    wave = np.where(slot <= L // 2, slot, sine_wave(slot))
    angle = 2.0 * np.pi / L * (wave * site % L)
    basis = np.where(slot <= L // 2, np.cos(angle), np.sin(angle)) * np.sqrt(2.0)
    basis[0] = 1.0
    basis[L // 2] = np.cos(np.pi * np.arange(L))
    return basis / np.sqrt(L)


def tables():
    basis_x = real_basis(lambda slot: slot - L // 2)
    basis_k = real_basis(lambda slot: L - slot)
    along_x = np.einsum("ab,cd,mx->acxdbm", np.eye(2), np.eye(2), basis_x).reshape(256, 256)
    along_y = basis_k.reshape(16, 2, 2, 32, 2).transpose(2, 1, 0, 4, 3).reshape(64, 64)
    along_z = np.einsum("ab,kz->akzb", np.eye(2), basis_k).reshape(128, 128)
    return split_constant(along_x), split_constant(along_y), split_constant(along_z)


def split(value):
    high = value.astype(jnp.bfloat16)
    return high, (value - high.astype(jnp.float32)).astype(jnp.bfloat16)


def dot(a, b):
    return jnp.dot(a, b, preferred_element_type=jnp.float32)


def live_of(counts_ref, base):
    seen = jnp.int32(0)
    live = [jnp.int32(0)] * LIVE
    for j in range(PER):
        alive = counts_ref[base + j] > 0
        for k in range(LIVE):
            live[k] = jnp.where(alive & (seen == k), j, live[k])
        seen = seen + alive.astype(jnp.int32)
    return live


def planes(ref, *at):
    return [ref[(*at, pl.ds(z, ROWS, stride=DEPTH), slice(None))] for z in range(DEPTH)]


def beside(v, lane):
    swapped = pltpu.roll(v, L, axis=1)
    rows = v.shape[0]
    y = swapped + jnp.where(lane < L, pltpu.roll(swapped, 1, axis=0), pltpu.roll(swapped, rows - 1, axis=0))
    inner = lane & (L - 1)
    low = pltpu.roll(jnp.where(inner == L - 1, swapped, v), 1, axis=1)
    high = pltpu.roll(jnp.where(inner == 0, swapped, v), 127, axis=1)
    return y + (low + high)


KICK = float(np.sqrt(np.float32(0.2)))


def update(center, near, mass, noise_now, lane):
    near = near + beside(center, lane)
    return center * (0.4 - 0.1 * mass - 0.05 * (center * center)) + 0.1 * near + KICK * noise_now


def edges_kernel(base_ref, odd_ref, counts_ref, field, noise, masses, near_out, far_out, mid, fbuf, nbuf, mbuf, sems):
    odd = odd_ref[0] > 0
    live = live_of(counts_ref, base_ref[0])
    first = pltpu.make_async_copy(masses, mbuf, sems.at[2 * LIVE])
    first.start()
    copies = []
    for k in range(LIVE):
        copies.append(
            [
                pltpu.make_async_copy(field.at[live[k]], fbuf.at[k], sems.at[2 * k]),
                pltpu.make_async_copy(noise.at[0, live[k]], nbuf.at[k], sems.at[2 * k + 1]),
            ]
        )
        for copy in copies[-1]:
            copy.start()
    first.wait()
    lane = lax.broadcasted_iota(jnp.int32, (ROWS, 128), 1)
    mass = planes(mbuf)
    for k in range(LIVE):
        for copy in copies[k]:
            copy.wait()
        old = planes(fbuf, k)
        kicks = planes(nbuf, k)
        near = (old[1], old[0] + old[2], old[1] + old[3], old[2])
        new = [update(old[z], near[z], mass[z], kicks[z], lane) for z in range(DEPTH)]
        for i, value in ((0, old), (1, new)):
            near_out[2 * k + i] = jnp.where(odd, value[0], value[3])
            far_out[2 * k + i] = jnp.where(odd, value[3], value[0])
        mid[2 * k] = new[1]
        mid[2 * k + 1] = new[2]


def floor_div(value, by):
    return jnp.floor((value.astype(jnp.float32) + 0.5) * (1.0 / by)).astype(jnp.int32)


def plan_kernel(counts_ref, slots_ref, bins_ref, item_ref, wide_ref, map_ref):
    total = counts_ref.shape[1]
    row = lax.broadcasted_iota(jnp.int32, (total, total), 0)
    col = lax.broadcasted_iota(jnp.int32, (total, total), 1)
    number = jnp.broadcast_to(counts_ref[...].astype(jnp.float32), (total, total))
    slot = jnp.broadcast_to(slots_ref[...].astype(jnp.float32), (total, total))

    def along(mask, value):
        return jnp.sum(jnp.where(mask, value, 0.0), axis=1, keepdims=True)

    own = along(row == col, number)
    ends = along(col <= row, number)
    slot_column = along(row == col, slot)
    block_row = floor_div(row, PER)
    block_col = floor_div(col, PER)
    rank = along((block_row == block_col) & (col < row) & (number > 0.0), jnp.ones_like(number))
    name = rank + BLOCKS * block_row[:, :1].astype(jnp.float32)
    position = jnp.sum(
        jnp.where(slot_column == col.astype(jnp.float32), row.astype(jnp.float32), 0.0), axis=0, keepdims=True
    )
    held = (position >= ends - own) & (position < ends)
    item = jnp.sum(jnp.where(held, name, 0.0), axis=0, keepdims=True)
    item_ref[...] = item.astype(jnp.int32)
    devices = total // PER
    to = lax.broadcasted_iota(jnp.int32, (devices, total), 0)
    s = lax.broadcasted_iota(jnp.int32, (devices, total), 1)
    lane = lax.broadcasted_iota(jnp.int32, (devices, 128), 1)
    wide = jnp.full((devices, 128), -1.0, jnp.float32)
    items = jnp.broadcast_to(item, (devices, total))
    for q in range(PER):
        column = jnp.sum(jnp.where(s == to * PER + q, items, 0.0), axis=1, keepdims=True)
        wide = jnp.where((lane >= NBINS * q) & (lane < NBINS * (q + 1)), column, wide)
    wide_ref[...] = wide.astype(jnp.int32)
    lane = lax.broadcasted_iota(jnp.int32, (L, 128), 1)
    for pair in range(2):
        halves = []
        for odd in range(2):
            bins = bins_ref[2 * pair + odd]
            halves.append(jnp.where(lane <= L // 2, bins, pltpu.roll(bins, L // 2, axis=1)))
        map_ref[pair * L : (pair + 1) * L, :] = jnp.where(lane < L, halves[0], pltpu.roll(halves[1], L, axis=1))


def sweep_kernel(
    base_ref,
    odd_ref,
    counts_ref,
    noise,
    masses,
    near_in,
    far_in,
    near_own,
    far_own,
    mid,
    along_x,
    along_y,
    pieces,
    chunks,
    nbuf,
    mbuf,
    sems,
):
    odd = odd_ref[0] > 0
    live = live_of(counts_ref, base_ref[0])
    first = pltpu.make_async_copy(masses, mbuf, sems.at[LIVE])
    first.start()
    copies = [pltpu.make_async_copy(noise.at[1, live[k]], nbuf.at[k], sems.at[k]) for k in range(LIVE)]
    for copy in copies:
        copy.start()
    first.wait()
    lane = lax.broadcasted_iota(jnp.int32, (ROWS, 128), 1)
    mass = planes(mbuf)
    left = []
    for k in range(LIVE):
        copies[k].wait()
        beyond = [t[2 * k + 1] + 0.1 * own[2 * k] for t, own in ((near_in, near_own), (far_in, far_own))]
        within = [own[2 * k + 1] + 0.1 * t[2 * k] for t, own in ((near_in, near_own), (far_in, far_own))]
        now = [
            jnp.where(odd, beyond[0], beyond[1]),
            jnp.where(odd, within[0], within[1]),
            mid[2 * k],
            mid[2 * k + 1],
            jnp.where(odd, within[1], within[0]),
            jnp.where(odd, beyond[1], beyond[0]),
        ]
        kicks = planes(nbuf, k)
        new = [update(now[p + 1], now[p] + now[p + 2], mass[p], kicks[p], lane) for p in range(DEPTH)]
        for z in range(DEPTH):
            pieces[pl.ds(k * DEPTH + z, ROWS, stride=BLOCKS * DEPTH), :] = new[z]
        left += [jnp.concatenate(new[0:2], axis=1), jnp.concatenate(new[2:4], axis=1)]
    high, low = split(jnp.concatenate(left, axis=0))
    across = dot(high, along_x[0]) + (dot(low, along_x[0]) + dot(high, along_x[1]))
    parts = [across[i * ROWS : (i + 1) * ROWS] for i in range(2 * LIVE)]
    right = jnp.concatenate([jnp.concatenate([p[:, :128], p[:, 128:]], axis=0) for p in parts], axis=1)
    high, low = split(right)
    turned = dot(along_y[0], high) + (dot(along_y[0], low) + dot(along_y[1], high))
    for i in range(2 * LIVE):
        even = turned[:ROWS, 128 * i : 128 * (i + 1)]
        odd = turned[ROWS:, 128 * i : 128 * (i + 1)]
        ready = (
            jnp.where(lane < L, even, pltpu.roll(odd, L, axis=1)),
            jnp.where(lane < L, pltpu.roll(even, L, axis=1), odd),
        )
        for side in range(2):
            for pair in range(2):
                chunks[pl.ds(i * 4 + side * 2 + pair, 16, stride=8 * LIVE), :] = ready[side][16 * pair : 16 * pair + 16]


def bins_kernel(me_ref, chunks, map_ref, wide, along_z, _, pieces, rows, block, sem):
    devices = wide.shape[0]
    place = map_ref[...]
    power = []
    for k in range(LIVE):
        high, low = split(chunks[:, 8 * k : 8 * k + 8, :].reshape(128, 128))
        mode = dot(along_z[0], high) + (dot(along_z[0], low) + dot(along_z[1], high))
        power.append(mode * mode)
    power.append(jnp.ones_like(power[0]))
    for b in range(NBINS):
        here = place == b
        for k in range(BLOCKS):
            rows[k * NBINS + b : k * NBINS + b + 1, :] = jnp.sum(
                jnp.where(here, power[k], 0.0), axis=0, keepdims=True
            )
    rows[BLOCKS * NBINS :, :] = jnp.zeros((128 - BLOCKS * NBINS, 128), jnp.float32)
    sums = lax.dot_general(
        jnp.ones((8, 128), jnp.float32),
        rows[...],
        (((1,), (1,)), ((), ())),
        precision=lax.Precision.HIGHEST,
        preferred_element_type=jnp.float32,
    )[0:1]
    lane = lax.broadcasted_iota(jnp.int32, (1, 128), 1)
    mine = jnp.where(lane >= NBINS * PER, spread(sums, LIVE, lane) * (1.0 / devices), 0.0)
    mine = jnp.broadcast_to(mine, (devices, 128))
    for k in range(LIVE):
        mine = jnp.where(wide[...] == me_ref[0] * BLOCKS + k, spread(sums, k, lane), mine)
    for d in range(devices):
        block[d] = jnp.broadcast_to(mine[d : d + 1], (DEPTH, 128))
    copy = pltpu.make_async_copy(block, pieces.at[:, LIVE], sem)
    copy.start()
    copy.wait()


def spread(row, k, lane):
    row = jnp.where((lane >= NBINS * k) & (lane < NBINS * (k + 1)), row, 0.0)
    for shift in (16, 32, 64):
        row = row + pltpu.roll(row, shift, axis=1)
    return row


def pick_kernel(item_ref, pieces, out, part):
    devices = pieces.shape[0] // BLOCKS
    for s in range(devices * PER):
        out[s] = pieces[item_ref[s]]
    sums = pieces[LIVE]
    for d in range(1, devices):
        sums = sums + pieces[d * BLOCKS + LIVE]
    part[...] = sums[0:1]


def finish_kernel(got, sums_ref, resampled, propagator):
    devices = got.shape[0] // PER
    for q in range(PER):
        for d in range(devices):
            resampled[q, :, 128 * d : 128 * (d + 1)] = got[d * PER + q]
    lane = lax.broadcasted_iota(jnp.int32, (1, 128), 1)
    ratio = sums_ref[...] / spread(sums_ref[...], PER, lane)
    for q in range(PER):
        turned = ratio if q == 0 else pltpu.roll(ratio, 128 - NBINS * q, axis=1)
        propagator[q : q + 1, :] = turned[:, :NBINS]


def spec(space):
    return pl.BlockSpec(memory_space=space)


def shape(*dims, dtype=jnp.float32):
    return jax.ShapeDtypeStruct(dims, dtype)


def rows_view(slabs):
    lead = slabs.shape[:-2]
    parts = slabs.reshape(*lead, DEPTH, ROWS, 128)
    return jnp.swapaxes(parts, -3, -2).reshape(*lead, DEPTH * ROWS, 128)


def edges(base, odd, counts, field, noise, masses):
    return pl.pallas_call(
        edges_kernel,
        out_shape=[shape(2 * LIVE, ROWS, 128)] * 3,
        in_specs=[spec(SMEM)] * 3 + [spec(pl.ANY)] * 3,
        out_specs=[spec(VMEM)] * 3,
        scratch_shapes=[
            VMEM((LIVE, 128, 128), jnp.float32),
            VMEM((LIVE, 128, 128), jnp.float32),
            VMEM((128, 128), jnp.float32),
            pltpu.SemaphoreType.DMA((2 * LIVE + 1,)),
        ],
        name="edges",
    )(base, odd, counts, field, noise, masses)


def plan(counts, dest_slots, mode_bins):
    total = counts.shape[0]
    padded = jnp.pad(mode_bins, ((0, 0), (0, 0), (0, 128 - mode_bins.shape[2])))
    return pl.pallas_call(
        plan_kernel,
        out_shape=[
            shape(1, total, dtype=jnp.int32),
            shape(total // PER, 128, dtype=jnp.int32),
            shape(128, 128, dtype=jnp.int32),
        ],
        in_specs=[spec(VMEM)] * 3,
        out_specs=[spec(VMEM)] * 3,
        compiler_params=pltpu.CompilerParams(vmem_limit_bytes=GRANT),
        name="plan",
    )(counts.reshape(1, total), dest_slots.reshape(1, total), padded)


def sweeps(base, odd, counts, noise, masses, *blocks):
    return pl.pallas_call(
        sweep_kernel,
        out_shape=[shape(ROWS * BLOCKS * DEPTH, 128), shape(16 * 8 * LIVE, 128)],
        in_specs=[spec(SMEM)] * 3 + [spec(pl.ANY)] * 2 + [spec(VMEM)] * 7,
        out_specs=[spec(VMEM)] * 2,
        scratch_shapes=[
            VMEM((LIVE, 128, 128), jnp.float32),
            VMEM((128, 128), jnp.float32),
            pltpu.SemaphoreType.DMA((LIVE + 1,)),
        ],
        compiler_params=pltpu.CompilerParams(vmem_limit_bytes=GRANT),
        name="sweeps",
    )(base, odd, counts, noise, masses, *blocks)


def bins(me, chunks, place, wide, along_z, pieces):
    devices = wide.shape[0]
    return pl.pallas_call(
        bins_kernel,
        out_shape=shape(devices, BLOCKS, DEPTH, 128),
        in_specs=[spec(SMEM)] + [spec(VMEM)] * 4 + [spec(pl.ANY)],
        out_specs=spec(pl.ANY),
        scratch_shapes=[
            VMEM((128, 128), jnp.float32),
            VMEM((devices, DEPTH, 128), jnp.float32),
            pltpu.SemaphoreType.DMA,
        ],
        input_output_aliases={5: 0},
        compiler_params=pltpu.CompilerParams(vmem_limit_bytes=GRANT),
        name="bins",
    )(me, chunks, place, wide, along_z, pieces)


def pick(item, pieces):
    return pl.pallas_call(
        pick_kernel,
        out_shape=[shape(item.shape[0], DEPTH, 128), shape(1, 128)],
        in_specs=[spec(SMEM), spec(VMEM)],
        out_specs=[spec(VMEM)] * 2,
        compiler_params=pltpu.CompilerParams(vmem_limit_bytes=GRANT),
        name="pick",
    )(item, pieces)


def finish(got, sums):
    return pl.pallas_call(
        finish_kernel,
        out_shape=[shape(PER, DEPTH, L * L), shape(PER, NBINS)],
        in_specs=[spec(VMEM)] * 2,
        out_specs=[spec(VMEM)] * 2,
        compiler_params=pltpu.CompilerParams(vmem_limit_bytes=GRANT),
        name="finish",
    )(got, sums)


def local(lattice_field, langevin_noise, masses, counts, dest_slots, mode_bins):
    along_x, along_y, along_z = (jnp.asarray(t) for t in tables())
    me = lax.axis_index("rep").astype(jnp.int32).reshape(1)
    base = me * PER
    field, noise, mass = rows_view(lattice_field), rows_view(langevin_noise), rows_view(masses)
    odd = (lax.axis_index("gz").astype(jnp.int32) & 1).reshape(1)
    near, far, mid = edges(base, odd, counts, field, noise, mass)
    ring = lax.axis_size("gz")
    near_in = lax.ppermute(near, "gz", [(i, i ^ 1) for i in range(ring)])
    far_in = lax.ppermute(far, "gz", [(i, (i + 1) % ring if i % 2 else (i - 1) % ring) for i in range(ring)])
    far_in, near_in, item, wide, place = lax.optimization_barrier(
        (far_in, near_in, *plan(counts, dest_slots, mode_bins))
    )
    pieces, chunks = sweeps(base, odd, counts, noise, mass, near_in, far_in, near, far, mid, along_x, along_y)
    reps = lax.axis_size("rep")
    chunks = lax.all_to_all(chunks.reshape(ring, 8 * LIVE, 128), "gz", 0, 0, tiled=True)
    pieces = bins(me, chunks, place, wide, along_z, pieces.reshape(reps, BLOCKS, DEPTH, 128))
    pieces = lax.all_to_all(pieces, "rep", 0, 0, tiled=True)
    out, sums = pick(item.reshape(-1), pieces.reshape(reps * BLOCKS, DEPTH, 128))
    got = lax.all_to_all(out.reshape(reps, PER, DEPTH, 128), "rep", 0, 0, tiled=True)
    step = 1
    while step < ring:
        sums = sums + lax.ppermute(sums, "gz", [(i, i ^ step) for i in range(ring)])
        step *= 2
    resampled, propagator = finish(got.reshape(reps * PER, DEPTH, 128), sums)
    return resampled, propagator


def solution(mesh):
    in_specs = (
        P("rep", "gz", None),
        P(None, "rep", "gz", None),
        P("gz", None),
        P(),
        P(),
        P("gz", None, None),
    )
    out_specs = (P("rep", "gz", None), P("rep", None))
    return jax.shard_map(local, mesh=mesh, in_specs=in_specs, out_specs=out_specs, check_vma=False)
```

```python
import jax
import jax.numpy as jnp
import ml_dtypes
import numpy as np
from jax import lax
from jax.experimental import pallas as pl
from jax.experimental.pallas import tpu as pltpu
from jax.sharding import PartitionSpec as P

L = 64
NBINS = 16
LIVE = 3
DEPTH = 4
ROWS = 32
PER = 6
BLOCKS = LIVE + 1
GRANT = 8 << 20

VMEM = pltpu.VMEM
SMEM = pltpu.SMEM


def split_constant(table):
    table = table.astype(np.float32)
    high = table.astype(ml_dtypes.bfloat16)
    low = (table - high.astype(np.float32)).astype(ml_dtypes.bfloat16)
    return np.stack([high, low])


def real_basis(sine_wave):
    slot = np.arange(L)[:, None]
    site = np.arange(L)[None, :]
    wave = np.where(slot <= L // 2, slot, sine_wave(slot))
    angle = 2.0 * np.pi / L * (wave * site % L)
    basis = np.where(slot <= L // 2, np.cos(angle), np.sin(angle)) * np.sqrt(2.0)
    basis[0] = 1.0
    basis[L // 2] = np.cos(np.pi * np.arange(L))
    return basis / np.sqrt(L)


def tables():
    basis_x = real_basis(lambda slot: slot - L // 2)
    basis_k = real_basis(lambda slot: L - slot)
    along_x = np.einsum("ab,cd,mx->acxdbm", np.eye(2), np.eye(2), basis_x).reshape(256, 256)
    along_y = basis_k.reshape(16, 2, 2, 32, 2).transpose(2, 1, 0, 4, 3).reshape(64, 64)
    along_z = np.einsum("ab,kz->akzb", np.eye(2), basis_k).reshape(128, 128)
    return split_constant(along_x), split_constant(along_y), split_constant(along_z)


def split(value):
    high = value.astype(jnp.bfloat16)
    return high, (value - high.astype(jnp.float32)).astype(jnp.bfloat16)


def dot(a, b):
    return jnp.dot(a, b, preferred_element_type=jnp.float32)


def live_of(counts_ref, base):
    seen = jnp.int32(0)
    live = [jnp.int32(0)] * LIVE
    for j in range(PER):
        alive = counts_ref[base + j] > 0
        for k in range(LIVE):
            live[k] = jnp.where(alive & (seen == k), j, live[k])
        seen = seen + alive.astype(jnp.int32)
    return live


def planes(ref, *at):
    return [ref[(*at, pl.ds(z, ROWS, stride=DEPTH), slice(None))] for z in range(DEPTH)]


def beside(v, lane):
    swapped = pltpu.roll(v, L, axis=1)
    rows = v.shape[0]
    y = swapped + jnp.where(lane < L, pltpu.roll(swapped, 1, axis=0), pltpu.roll(swapped, rows - 1, axis=0))
    inner = lane & (L - 1)
    low = pltpu.roll(jnp.where(inner == L - 1, swapped, v), 1, axis=1)
    high = pltpu.roll(jnp.where(inner == 0, swapped, v), 127, axis=1)
    return y + (low + high)


KICK = float(np.sqrt(np.float32(0.2)))


def update(center, near, mass, noise_now, lane):
    near = near + beside(center, lane)
    return center * (0.4 - 0.1 * mass - 0.05 * (center * center)) + 0.1 * near + KICK * noise_now


def edges_kernel(base_ref, odd_ref, counts_ref, field, noise, masses, near_out, far_out, mid, later, mbuf, fbuf, nbuf, sems):
    odd = odd_ref[0] > 0
    live = live_of(counts_ref, base_ref[0])
    first = pltpu.make_async_copy(masses, mbuf, sems.at[2 * LIVE])
    first.start()
    copies = []
    for k in range(LIVE):
        copies.append(
            [
                pltpu.make_async_copy(field.at[live[k]], fbuf.at[k], sems.at[2 * k]),
                pltpu.make_async_copy(noise.at[0, live[k]], nbuf.at[k], sems.at[2 * k + 1]),
            ]
        )
        for copy in copies[-1]:
            copy.start()
    last = [pltpu.make_async_copy(noise.at[1, live[k]], later.at[k], sems.at[2 * LIVE + 1 + k]) for k in range(LIVE)]
    for copy in last:
        copy.start()
    first.wait()
    lane = lax.broadcasted_iota(jnp.int32, (ROWS, 128), 1)
    mass = planes(mbuf)
    for k in range(LIVE):
        for copy in copies[k]:
            copy.wait()
        old = planes(fbuf, k)
        kicks = planes(nbuf, k)
        near = (old[1], old[0] + old[2], old[1] + old[3], old[2])
        new = [update(old[z], near[z], mass[z], kicks[z], lane) for z in range(DEPTH)]
        for i, value in ((0, old), (1, new)):
            near_out[2 * k + i] = jnp.where(odd, value[0], value[3])
            far_out[2 * k + i] = jnp.where(odd, value[3], value[0])
        mid[2 * k] = new[1]
        mid[2 * k + 1] = new[2]
    for copy in last:
        copy.wait()


def floor_div(value, by):
    return jnp.floor((value.astype(jnp.float32) + 0.5) * (1.0 / by)).astype(jnp.int32)


def plan_kernel(counts_ref, slots_ref, bins_ref, item_ref, wide_ref, map_ref):
    total = counts_ref.shape[1]
    row = lax.broadcasted_iota(jnp.int32, (total, total), 0)
    col = lax.broadcasted_iota(jnp.int32, (total, total), 1)
    number = jnp.broadcast_to(counts_ref[...].astype(jnp.float32), (total, total))
    slot = jnp.broadcast_to(slots_ref[...].astype(jnp.float32), (total, total))

    def along(mask, value):
        return jnp.sum(jnp.where(mask, value, 0.0), axis=1, keepdims=True)

    own = along(row == col, number)
    ends = along(col <= row, number)
    slot_column = along(row == col, slot)
    block_row = floor_div(row, PER)
    block_col = floor_div(col, PER)
    rank = along((block_row == block_col) & (col < row) & (number > 0.0), jnp.ones_like(number))
    name = rank + BLOCKS * block_row[:, :1].astype(jnp.float32)
    position = jnp.sum(
        jnp.where(slot_column == col.astype(jnp.float32), row.astype(jnp.float32), 0.0), axis=0, keepdims=True
    )
    held = (position >= ends - own) & (position < ends)
    item = jnp.sum(jnp.where(held, name, 0.0), axis=0, keepdims=True)
    item_ref[...] = item.astype(jnp.int32)
    devices = total // PER
    to = lax.broadcasted_iota(jnp.int32, (devices, total), 0)
    s = lax.broadcasted_iota(jnp.int32, (devices, total), 1)
    lane = lax.broadcasted_iota(jnp.int32, (devices, 128), 1)
    wide = jnp.full((devices, 128), -1.0, jnp.float32)
    items = jnp.broadcast_to(item, (devices, total))
    for q in range(PER):
        column = jnp.sum(jnp.where(s == to * PER + q, items, 0.0), axis=1, keepdims=True)
        wide = jnp.where((lane >= NBINS * q) & (lane < NBINS * (q + 1)), column, wide)
    wide_ref[...] = wide.astype(jnp.int32)
    lane = lax.broadcasted_iota(jnp.int32, (L, 128), 1)
    for pair in range(2):
        halves = []
        for odd in range(2):
            bins = bins_ref[2 * pair + odd]
            halves.append(jnp.where(lane <= L // 2, bins, pltpu.roll(bins, L // 2, axis=1)))
        map_ref[pair * L : (pair + 1) * L, :] = jnp.where(lane < L, halves[0], pltpu.roll(halves[1], L, axis=1))


def sweep_kernel(
    odd_ref, near_in, far_in, near_own, far_own, mid, later, masses, along_x, along_y, pieces, chunks
):
    odd = odd_ref[0] > 0
    lane = lax.broadcasted_iota(jnp.int32, (ROWS, 128), 1)
    mass = planes(masses)
    left = []
    for k in range(LIVE):
        beyond = [t[2 * k + 1] + 0.1 * own[2 * k] for t, own in ((near_in, near_own), (far_in, far_own))]
        within = [own[2 * k + 1] + 0.1 * t[2 * k] for t, own in ((near_in, near_own), (far_in, far_own))]
        now = [
            jnp.where(odd, beyond[0], beyond[1]),
            jnp.where(odd, within[0], within[1]),
            mid[2 * k],
            mid[2 * k + 1],
            jnp.where(odd, within[1], within[0]),
            jnp.where(odd, beyond[1], beyond[0]),
        ]
        kicks = planes(later, k)
        new = [update(now[p + 1], now[p] + now[p + 2], mass[p], kicks[p], lane) for p in range(DEPTH)]
        for z in range(DEPTH):
            pieces[pl.ds(k * DEPTH + z, ROWS, stride=BLOCKS * DEPTH), :] = new[z]
        left += [jnp.concatenate(new[0:2], axis=1), jnp.concatenate(new[2:4], axis=1)]
    high, low = split(jnp.concatenate(left, axis=0))
    across = dot(high, along_x[0]) + (dot(low, along_x[0]) + dot(high, along_x[1]))
    parts = [across[i * ROWS : (i + 1) * ROWS] for i in range(2 * LIVE)]
    right = jnp.concatenate([jnp.concatenate([p[:, :128], p[:, 128:]], axis=0) for p in parts], axis=1)
    high, low = split(right)
    turned = dot(along_y[0], high) + (dot(along_y[0], low) + dot(along_y[1], high))
    for i in range(2 * LIVE):
        even = turned[:ROWS, 128 * i : 128 * (i + 1)]
        odd = turned[ROWS:, 128 * i : 128 * (i + 1)]
        ready = (
            jnp.where(lane < L, even, pltpu.roll(odd, L, axis=1)),
            jnp.where(lane < L, pltpu.roll(even, L, axis=1), odd),
        )
        for side in range(2):
            for pair in range(2):
                chunks[pl.ds(i * 4 + side * 2 + pair, 16, stride=8 * LIVE), :] = ready[side][16 * pair : 16 * pair + 16]


def bins_kernel(me_ref, chunks, map_ref, wide, along_z, _, pieces, rows, block, sem):
    devices = wide.shape[0]
    place = map_ref[...]
    power = []
    for k in range(LIVE):
        high, low = split(chunks[:, 8 * k : 8 * k + 8, :].reshape(128, 128))
        mode = dot(along_z[0], high) + (dot(along_z[0], low) + dot(along_z[1], high))
        power.append(mode * mode)
    power.append(jnp.ones_like(power[0]))
    for b in range(NBINS):
        here = place == b
        for k in range(BLOCKS):
            rows[k * NBINS + b : k * NBINS + b + 1, :] = jnp.sum(
                jnp.where(here, power[k], 0.0), axis=0, keepdims=True
            )
    rows[BLOCKS * NBINS :, :] = jnp.zeros((128 - BLOCKS * NBINS, 128), jnp.float32)
    sums = lax.dot_general(
        jnp.ones((8, 128), jnp.float32),
        rows[...],
        (((1,), (1,)), ((), ())),
        precision=lax.Precision.HIGHEST,
        preferred_element_type=jnp.float32,
    )[0:1]
    lane = lax.broadcasted_iota(jnp.int32, (1, 128), 1)
    mine = jnp.where(lane >= NBINS * PER, spread(sums, LIVE, lane) * (1.0 / devices), 0.0)
    mine = jnp.broadcast_to(mine, (devices, 128))
    for k in range(LIVE):
        mine = jnp.where(wide[...] == me_ref[0] * BLOCKS + k, spread(sums, k, lane), mine)
    for d in range(devices):
        block[d] = jnp.broadcast_to(mine[d : d + 1], (DEPTH, 128))
    copy = pltpu.make_async_copy(block, pieces.at[:, LIVE], sem)
    copy.start()
    copy.wait()


def spread(row, k, lane):
    row = jnp.where((lane >= NBINS * k) & (lane < NBINS * (k + 1)), row, 0.0)
    for shift in (16, 32, 64):
        row = row + pltpu.roll(row, shift, axis=1)
    return row


def pick_kernel(item_ref, pieces, out, part):
    devices = pieces.shape[0] // BLOCKS
    for s in range(devices * PER):
        out[s] = pieces[item_ref[s]]
    sums = pieces[LIVE]
    for d in range(1, devices):
        sums = sums + pieces[d * BLOCKS + LIVE]
    part[...] = sums[0:1]


def finish_kernel(got, sums_ref, resampled, propagator):
    devices = got.shape[0] // PER
    for q in range(PER):
        for d in range(devices):
            resampled[q, :, 128 * d : 128 * (d + 1)] = got[d * PER + q]
    lane = lax.broadcasted_iota(jnp.int32, (1, 128), 1)
    ratio = sums_ref[...] / spread(sums_ref[...], PER, lane)
    for q in range(PER):
        turned = ratio if q == 0 else pltpu.roll(ratio, 128 - NBINS * q, axis=1)
        propagator[q : q + 1, :] = turned[:, :NBINS]


def spec(space):
    return pl.BlockSpec(memory_space=space)


def shape(*dims, dtype=jnp.float32):
    return jax.ShapeDtypeStruct(dims, dtype)


def rows_view(slabs):
    lead = slabs.shape[:-2]
    parts = slabs.reshape(*lead, DEPTH, ROWS, 128)
    return jnp.swapaxes(parts, -3, -2).reshape(*lead, DEPTH * ROWS, 128)


def edges(base, odd, counts, field, noise, masses):
    return pl.pallas_call(
        edges_kernel,
        out_shape=[shape(2 * LIVE, ROWS, 128)] * 3 + [shape(LIVE, 128, 128), shape(128, 128)],
        in_specs=[spec(SMEM)] * 3 + [spec(pl.ANY)] * 3,
        out_specs=[spec(VMEM)] * 5,
        scratch_shapes=[
            VMEM((LIVE, 128, 128), jnp.float32),
            VMEM((LIVE, 128, 128), jnp.float32),
            pltpu.SemaphoreType.DMA((3 * LIVE + 1,)),
        ],
        compiler_params=pltpu.CompilerParams(vmem_limit_bytes=GRANT),
        name="edges",
    )(base, odd, counts, field, noise, masses)


def plan(counts, dest_slots, mode_bins):
    total = counts.shape[0]
    padded = jnp.pad(mode_bins, ((0, 0), (0, 0), (0, 128 - mode_bins.shape[2])))
    return pl.pallas_call(
        plan_kernel,
        out_shape=[
            shape(1, total, dtype=jnp.int32),
            shape(total // PER, 128, dtype=jnp.int32),
            shape(128, 128, dtype=jnp.int32),
        ],
        in_specs=[spec(VMEM)] * 3,
        out_specs=[spec(VMEM)] * 3,
        compiler_params=pltpu.CompilerParams(vmem_limit_bytes=GRANT),
        name="plan",
    )(counts.reshape(1, total), dest_slots.reshape(1, total), padded)


def sweeps(*blocks):
    return pl.pallas_call(
        sweep_kernel,
        out_shape=[shape(ROWS * BLOCKS * DEPTH, 128), shape(16 * 8 * LIVE, 128)],
        in_specs=[spec(SMEM)] + [spec(VMEM)] * 9,
        out_specs=[spec(VMEM)] * 2,
        compiler_params=pltpu.CompilerParams(vmem_limit_bytes=GRANT),
        name="sweeps",
    )(*blocks)


def bins(me, chunks, place, wide, along_z, pieces):
    devices = wide.shape[0]
    return pl.pallas_call(
        bins_kernel,
        out_shape=shape(devices, BLOCKS, DEPTH, 128),
        in_specs=[spec(SMEM)] + [spec(VMEM)] * 4 + [spec(pl.ANY)],
        out_specs=spec(pl.ANY),
        scratch_shapes=[
            VMEM((128, 128), jnp.float32),
            VMEM((devices, DEPTH, 128), jnp.float32),
            pltpu.SemaphoreType.DMA,
        ],
        input_output_aliases={5: 0},
        compiler_params=pltpu.CompilerParams(vmem_limit_bytes=GRANT),
        name="bins",
    )(me, chunks, place, wide, along_z, pieces)


def pick(item, pieces):
    return pl.pallas_call(
        pick_kernel,
        out_shape=[shape(item.shape[0], DEPTH, 128), shape(1, 128)],
        in_specs=[spec(SMEM), spec(VMEM)],
        out_specs=[spec(VMEM)] * 2,
        compiler_params=pltpu.CompilerParams(vmem_limit_bytes=GRANT),
        name="pick",
    )(item, pieces)


def finish(got, sums):
    return pl.pallas_call(
        finish_kernel,
        out_shape=[shape(PER, DEPTH, L * L), shape(PER, NBINS)],
        in_specs=[spec(VMEM)] * 2,
        out_specs=[spec(VMEM)] * 2,
        compiler_params=pltpu.CompilerParams(vmem_limit_bytes=GRANT),
        name="finish",
    )(got, sums)


def local(lattice_field, langevin_noise, masses, counts, dest_slots, mode_bins):
    along_x, along_y, along_z = (jnp.asarray(t) for t in tables())
    me = lax.axis_index("rep").astype(jnp.int32).reshape(1)
    base = me * PER
    field, noise, mass = rows_view(lattice_field), rows_view(langevin_noise), rows_view(masses)
    odd = (lax.axis_index("gz").astype(jnp.int32) & 1).reshape(1)
    held = (pltpu.with_memory_space_constraint(a, pltpu.HBM) for a in (counts, field, noise, mass))
    near, far, mid, later, mass = edges(base, odd, *held)
    ring = lax.axis_size("gz")
    near_in = lax.ppermute(near, "gz", [(i, i ^ 1) for i in range(ring)])
    far_in = lax.ppermute(far, "gz", [(i, (i + 1) % ring if i % 2 else (i - 1) % ring) for i in range(ring)])
    far_in, near_in, item, wide, place = lax.optimization_barrier(
        (far_in, near_in, *plan(counts, dest_slots, mode_bins))
    )
    pieces, chunks = sweeps(odd, near_in, far_in, near, far, mid, later, mass, along_x, along_y)
    reps = lax.axis_size("rep")
    chunks = lax.all_to_all(chunks.reshape(ring, 8 * LIVE, 128), "gz", 0, 0, tiled=True)
    pieces = bins(me, chunks, place, wide, along_z, pieces.reshape(reps, BLOCKS, DEPTH, 128))
    pieces = lax.all_to_all(pieces, "rep", 0, 0, tiled=True)
    out, sums = pick(item.reshape(-1), pieces.reshape(reps * BLOCKS, DEPTH, 128))
    got = lax.all_to_all(out.reshape(reps, PER, DEPTH, 128), "rep", 0, 0, tiled=True)
    step = 1
    while step < ring:
        sums = sums + lax.ppermute(sums, "gz", [(i, i ^ step) for i in range(ring)])
        step *= 2
    resampled, propagator = finish(got.reshape(reps * PER, DEPTH, 128), sums)
    return resampled, propagator


def solution(mesh):
    in_specs = (
        P("rep", "gz", None),
        P(None, "rep", "gz", None),
        P("gz", None),
        P(),
        P(),
        P("gz", None, None),
    )
    out_specs = (P("rep", "gz", None), P("rep", None))
    return jax.shard_map(local, mesh=mesh, in_specs=in_specs, out_specs=out_specs, check_vma=False)
```

```python
import jax
import jax.numpy as jnp
import ml_dtypes
import numpy as np
from jax import lax
from jax.experimental import pallas as pl
from jax.experimental.pallas import tpu as pltpu
from jax.sharding import PartitionSpec as P

L = 64
NBINS = 16
LIVE = 3
DEPTH = 4
ROWS = 32
PER = 6
BLOCKS = LIVE + 1
SPAN = LIVE * DEPTH + 1
GRANT = 8 << 20

VMEM = pltpu.VMEM
SMEM = pltpu.SMEM


def split_constant(table):
    table = table.astype(np.float32)
    high = table.astype(ml_dtypes.bfloat16)
    low = (table - high.astype(np.float32)).astype(ml_dtypes.bfloat16)
    return np.stack([high, low])


def real_basis(sine_wave):
    slot = np.arange(L)[:, None]
    site = np.arange(L)[None, :]
    wave = np.where(slot <= L // 2, slot, sine_wave(slot))
    angle = 2.0 * np.pi / L * (wave * site % L)
    basis = np.where(slot <= L // 2, np.cos(angle), np.sin(angle)) * np.sqrt(2.0)
    basis[0] = 1.0
    basis[L // 2] = np.cos(np.pi * np.arange(L))
    return basis / np.sqrt(L)


def tables():
    basis_x = real_basis(lambda slot: slot - L // 2)
    basis_k = real_basis(lambda slot: L - slot)
    along_x = np.einsum("ab,cd,mx->acxdbm", np.eye(2), np.eye(2), basis_x).reshape(256, 256)
    along_y = basis_k.reshape(16, 2, 2, 32, 2).transpose(2, 1, 0, 4, 3).reshape(64, 64)
    along_z = np.einsum("ab,kz->akzb", np.eye(2), basis_k).reshape(128, 128)
    return split_constant(along_x), split_constant(along_y), split_constant(along_z)


def split(value):
    high = value.astype(jnp.bfloat16)
    return high, (value - high.astype(jnp.float32)).astype(jnp.bfloat16)


def dot(a, b):
    return jnp.dot(a, b, preferred_element_type=jnp.float32)


def live_of(counts_ref, base):
    seen = jnp.int32(0)
    live = [jnp.int32(0)] * LIVE
    for j in range(PER):
        alive = counts_ref[base + j] > 0
        for k in range(LIVE):
            live[k] = jnp.where(alive & (seen == k), j, live[k])
        seen = seen + alive.astype(jnp.int32)
    return live


def planes(ref, *at):
    return [ref[(*at, pl.ds(z, ROWS, stride=DEPTH), slice(None))] for z in range(DEPTH)]


def beside(v, lane):
    swapped = pltpu.roll(v, L, axis=1)
    rows = v.shape[0]
    y = swapped + jnp.where(lane < L, pltpu.roll(swapped, 1, axis=0), pltpu.roll(swapped, rows - 1, axis=0))
    inner = lane & (L - 1)
    low = pltpu.roll(jnp.where(inner == L - 1, swapped, v), 1, axis=1)
    high = pltpu.roll(jnp.where(inner == 0, swapped, v), 127, axis=1)
    return y + (low + high)


KICK = float(np.sqrt(np.float32(0.2)))


def update(center, near, mass, noise_now, lane):
    near = near + beside(center, lane)
    return center * (0.4 - 0.1 * mass - 0.05 * (center * center)) + 0.1 * near + KICK * noise_now


def edges_kernel(base_ref, odd_ref, counts_ref, field, noise, masses, near_out, far_out, mid, later, mbuf, fbuf, nbuf, sems):
    odd = odd_ref[0] > 0
    live = live_of(counts_ref, base_ref[0])
    first = pltpu.make_async_copy(masses, mbuf, sems.at[2 * LIVE])
    first.start()
    copies = []
    for k in range(LIVE):
        copies.append(
            [
                pltpu.make_async_copy(field.at[live[k]], fbuf.at[k], sems.at[2 * k]),
                pltpu.make_async_copy(noise.at[0, live[k]], nbuf.at[k], sems.at[2 * k + 1]),
            ]
        )
        for copy in copies[-1]:
            copy.start()
    last = [pltpu.make_async_copy(noise.at[1, live[k]], later.at[k], sems.at[2 * LIVE + 1 + k]) for k in range(LIVE)]
    for copy in last:
        copy.start()
    first.wait()
    lane = lax.broadcasted_iota(jnp.int32, (ROWS, 128), 1)
    mass = planes(mbuf)
    for k in range(LIVE):
        for copy in copies[k]:
            copy.wait()
        old = planes(fbuf, k)
        kicks = planes(nbuf, k)
        near = (old[1], old[0] + old[2], old[1] + old[3], old[2])
        new = [update(old[z], near[z], mass[z], kicks[z], lane) for z in range(DEPTH)]
        for i, value in ((0, old), (1, new)):
            near_out[2 * k + i] = jnp.where(odd, value[0], value[3])
            far_out[2 * k + i] = jnp.where(odd, value[3], value[0])
        mid[2 * k] = new[1]
        mid[2 * k + 1] = new[2]
    for copy in last:
        copy.wait()


def floor_div(value, by):
    return jnp.floor((value.astype(jnp.float32) + 0.5) * (1.0 / by)).astype(jnp.int32)


def plan_kernel(counts_ref, slots_ref, bins_ref, item_ref, wide_ref, map_ref):
    total = counts_ref.shape[1]
    row = lax.broadcasted_iota(jnp.int32, (total, total), 0)
    col = lax.broadcasted_iota(jnp.int32, (total, total), 1)
    number = jnp.broadcast_to(counts_ref[...].astype(jnp.float32), (total, total))
    slot = jnp.broadcast_to(slots_ref[...].astype(jnp.float32), (total, total))

    def along(mask, value):
        return jnp.sum(jnp.where(mask, value, 0.0), axis=1, keepdims=True)

    own = along(row == col, number)
    ends = along(col <= row, number)
    slot_column = along(row == col, slot)
    block_row = floor_div(row, PER)
    block_col = floor_div(col, PER)
    rank = along((block_row == block_col) & (col < row) & (number > 0.0), jnp.ones_like(number))
    name = DEPTH * rank + SPAN * block_row[:, :1].astype(jnp.float32)
    position = jnp.sum(
        jnp.where(slot_column == col.astype(jnp.float32), row.astype(jnp.float32), 0.0), axis=0, keepdims=True
    )
    held = (position >= ends - own) & (position < ends)
    item = jnp.sum(jnp.where(held, name, 0.0), axis=0, keepdims=True)
    item_ref[...] = item.astype(jnp.int32)
    devices = total // PER
    to = lax.broadcasted_iota(jnp.int32, (devices, total), 0)
    s = lax.broadcasted_iota(jnp.int32, (devices, total), 1)
    lane = lax.broadcasted_iota(jnp.int32, (devices, 128), 1)
    wide = jnp.full((devices, 128), -1.0, jnp.float32)
    items = jnp.broadcast_to(item, (devices, total))
    for q in range(PER):
        column = jnp.sum(jnp.where(s == to * PER + q, items, 0.0), axis=1, keepdims=True)
        wide = jnp.where((lane >= NBINS * q) & (lane < NBINS * (q + 1)), column, wide)
    wide_ref[...] = wide.astype(jnp.int32)
    lane = lax.broadcasted_iota(jnp.int32, (L, 128), 1)
    for pair in range(2):
        halves = []
        for odd in range(2):
            bins = bins_ref[2 * pair + odd]
            halves.append(jnp.where(lane <= L // 2, bins, pltpu.roll(bins, L // 2, axis=1)))
        map_ref[pair * L : (pair + 1) * L, :] = jnp.where(lane < L, halves[0], pltpu.roll(halves[1], L, axis=1))


def sweep_kernel(
    odd_ref, near_in, far_in, near_own, far_own, mid, later, masses, along_x, along_y, pieces, chunks
):
    odd = odd_ref[0] > 0
    lane = lax.broadcasted_iota(jnp.int32, (ROWS, 128), 1)
    mass = planes(masses)
    left = []
    for k in range(LIVE):
        beyond = [t[2 * k + 1] + 0.1 * own[2 * k] for t, own in ((near_in, near_own), (far_in, far_own))]
        within = [own[2 * k + 1] + 0.1 * t[2 * k] for t, own in ((near_in, near_own), (far_in, far_own))]
        now = [
            jnp.where(odd, beyond[0], beyond[1]),
            jnp.where(odd, within[0], within[1]),
            mid[2 * k],
            mid[2 * k + 1],
            jnp.where(odd, within[1], within[0]),
            jnp.where(odd, beyond[1], beyond[0]),
        ]
        kicks = planes(later, k)
        new = [update(now[p + 1], now[p] + now[p + 2], mass[p], kicks[p], lane) for p in range(DEPTH)]
        for z in range(DEPTH):
            pieces[pl.ds(k * DEPTH + z, ROWS, stride=SPAN), :] = new[z]
        left += [jnp.concatenate(new[0:2], axis=1), jnp.concatenate(new[2:4], axis=1)]
    high, low = split(jnp.concatenate(left, axis=0))
    across = dot(high, along_x[0]) + (dot(low, along_x[0]) + dot(high, along_x[1]))
    parts = [across[i * ROWS : (i + 1) * ROWS] for i in range(2 * LIVE)]
    right = jnp.concatenate([jnp.concatenate([p[:, :128], p[:, 128:]], axis=0) for p in parts], axis=1)
    high, low = split(right)
    turned = dot(along_y[0], high) + (dot(along_y[0], low) + dot(along_y[1], high))
    for i in range(2 * LIVE):
        even = turned[:ROWS, 128 * i : 128 * (i + 1)]
        odd = turned[ROWS:, 128 * i : 128 * (i + 1)]
        ready = (
            jnp.where(lane < L, even, pltpu.roll(odd, L, axis=1)),
            jnp.where(lane < L, pltpu.roll(even, L, axis=1), odd),
        )
        for side in range(2):
            for pair in range(2):
                chunks[pl.ds(i * 4 + side * 2 + pair, 16, stride=8 * LIVE), :] = ready[side][16 * pair : 16 * pair + 16]


def bins_kernel(me_ref, chunks, map_ref, wide, along_z, _, pieces, rows, block, sem):
    devices = wide.shape[0]
    place = map_ref[...]
    power = []
    for k in range(LIVE):
        high, low = split(chunks[:, 8 * k : 8 * k + 8, :].reshape(128, 128))
        mode = dot(along_z[0], high) + (dot(along_z[0], low) + dot(along_z[1], high))
        power.append(mode * mode)
    power.append(jnp.ones_like(power[0]))
    for b in range(NBINS):
        here = place == b
        for k in range(BLOCKS):
            rows[k * NBINS + b : k * NBINS + b + 1, :] = jnp.sum(
                jnp.where(here, power[k], 0.0), axis=0, keepdims=True
            )
    rows[BLOCKS * NBINS :, :] = jnp.zeros((128 - BLOCKS * NBINS, 128), jnp.float32)
    sums = lax.dot_general(
        jnp.ones((8, 128), jnp.float32),
        rows[...],
        (((1,), (1,)), ((), ())),
        precision=lax.Precision.HIGHEST,
        preferred_element_type=jnp.float32,
    )[0:1]
    lane = lax.broadcasted_iota(jnp.int32, (1, 128), 1)
    mine = jnp.where(lane >= NBINS * PER, spread(sums, LIVE, lane) * (1.0 / devices), 0.0)
    mine = jnp.broadcast_to(mine, (devices, 128))
    for k in range(LIVE):
        mine = jnp.where(wide[...] == me_ref[0] * SPAN + DEPTH * k, spread(sums, k, lane), mine)
    for d in range(devices):
        block[d] = mine[d : d + 1]
    copy = pltpu.make_async_copy(block, pieces.at[:, SPAN - 1], sem)
    copy.start()
    copy.wait()


def spread(row, k, lane):
    row = jnp.where((lane >= NBINS * k) & (lane < NBINS * (k + 1)), row, 0.0)
    for shift in (16, 32, 64):
        row = row + pltpu.roll(row, shift, axis=1)
    return row


def pick_kernel(item_ref, pieces, out, part):
    devices = pieces.shape[0] // SPAN
    for s in range(devices * PER):
        out[s] = pieces[pl.ds(item_ref[s], DEPTH), :]
    part[...] = jnp.sum(pieces[pl.ds(SPAN - 1, devices, stride=SPAN), :], axis=0, keepdims=True)


def finish_kernel(got, sums_ref, resampled, propagator):
    devices = got.shape[0] // PER
    for q in range(PER):
        for d in range(devices):
            resampled[q, :, 128 * d : 128 * (d + 1)] = got[d * PER + q]
    lane = lax.broadcasted_iota(jnp.int32, (1, 128), 1)
    ratio = sums_ref[...] / spread(sums_ref[...], PER, lane)
    for q in range(PER):
        turned = ratio if q == 0 else pltpu.roll(ratio, 128 - NBINS * q, axis=1)
        propagator[q : q + 1, :] = turned[:, :NBINS]


def spec(space):
    return pl.BlockSpec(memory_space=space)


def shape(*dims, dtype=jnp.float32):
    return jax.ShapeDtypeStruct(dims, dtype)


def rows_view(slabs):
    lead = slabs.shape[:-2]
    parts = slabs.reshape(*lead, DEPTH, ROWS, 128)
    return jnp.swapaxes(parts, -3, -2).reshape(*lead, DEPTH * ROWS, 128)


def edges(base, odd, counts, field, noise, masses):
    return pl.pallas_call(
        edges_kernel,
        out_shape=[shape(2 * LIVE, ROWS, 128)] * 3 + [shape(LIVE, 128, 128), shape(128, 128)],
        in_specs=[spec(SMEM)] * 3 + [spec(pl.ANY)] * 3,
        out_specs=[spec(VMEM)] * 5,
        scratch_shapes=[
            VMEM((LIVE, 128, 128), jnp.float32),
            VMEM((LIVE, 128, 128), jnp.float32),
            pltpu.SemaphoreType.DMA((3 * LIVE + 1,)),
        ],
        compiler_params=pltpu.CompilerParams(vmem_limit_bytes=GRANT),
        name="edges",
    )(base, odd, counts, field, noise, masses)


def plan(counts, dest_slots, mode_bins):
    total = counts.shape[0]
    padded = jnp.pad(mode_bins, ((0, 0), (0, 0), (0, 128 - mode_bins.shape[2])))
    return pl.pallas_call(
        plan_kernel,
        out_shape=[
            shape(1, total, dtype=jnp.int32),
            shape(total // PER, 128, dtype=jnp.int32),
            shape(128, 128, dtype=jnp.int32),
        ],
        in_specs=[spec(VMEM)] * 3,
        out_specs=[spec(VMEM)] * 3,
        compiler_params=pltpu.CompilerParams(vmem_limit_bytes=GRANT),
        name="plan",
    )(counts.reshape(1, total), dest_slots.reshape(1, total), padded)


def sweeps(*blocks):
    return pl.pallas_call(
        sweep_kernel,
        out_shape=[shape(ROWS * SPAN, 128), shape(16 * 8 * LIVE, 128)],
        in_specs=[spec(SMEM)] + [spec(VMEM)] * 9,
        out_specs=[spec(VMEM)] * 2,
        compiler_params=pltpu.CompilerParams(vmem_limit_bytes=GRANT),
        name="sweeps",
    )(*blocks)


def bins(me, chunks, place, wide, along_z, pieces):
    devices = wide.shape[0]
    return pl.pallas_call(
        bins_kernel,
        out_shape=shape(devices, SPAN, 1, 128),
        in_specs=[spec(SMEM)] + [spec(VMEM)] * 4 + [spec(pl.ANY)],
        out_specs=spec(pl.ANY),
        scratch_shapes=[
            VMEM((128, 128), jnp.float32),
            VMEM((devices, 1, 128), jnp.float32),
            pltpu.SemaphoreType.DMA,
        ],
        input_output_aliases={5: 0},
        compiler_params=pltpu.CompilerParams(vmem_limit_bytes=GRANT),
        name="bins",
    )(me, chunks, place, wide, along_z, pieces)


def pick(item, pieces):
    return pl.pallas_call(
        pick_kernel,
        out_shape=[shape(item.shape[0], DEPTH, 128), shape(1, 128)],
        in_specs=[spec(SMEM), spec(VMEM)],
        out_specs=[spec(VMEM)] * 2,
        compiler_params=pltpu.CompilerParams(vmem_limit_bytes=GRANT),
        name="pick",
    )(item, pieces)


def finish(got, sums):
    return pl.pallas_call(
        finish_kernel,
        out_shape=[shape(PER, DEPTH, L * L), shape(PER, NBINS)],
        in_specs=[spec(VMEM)] * 2,
        out_specs=[spec(VMEM)] * 2,
        compiler_params=pltpu.CompilerParams(vmem_limit_bytes=GRANT),
        name="finish",
    )(got, sums)


def local(lattice_field, langevin_noise, masses, counts, dest_slots, mode_bins):
    along_x, along_y, along_z = (jnp.asarray(t) for t in tables())
    me = lax.axis_index("rep").astype(jnp.int32).reshape(1)
    base = me * PER
    field, noise, mass = rows_view(lattice_field), rows_view(langevin_noise), rows_view(masses)
    odd = (lax.axis_index("gz").astype(jnp.int32) & 1).reshape(1)
    held = (pltpu.with_memory_space_constraint(a, pltpu.HBM) for a in (counts, field, noise, mass))
    near, far, mid, later, mass = edges(base, odd, *held)
    ring = lax.axis_size("gz")
    near_in = lax.ppermute(near, "gz", [(i, i ^ 1) for i in range(ring)])
    far_in = lax.ppermute(far, "gz", [(i, (i + 1) % ring if i % 2 else (i - 1) % ring) for i in range(ring)])
    far_in, near_in, item, wide, place = lax.optimization_barrier(
        (far_in, near_in, *plan(counts, dest_slots, mode_bins))
    )
    pieces, chunks = sweeps(odd, near_in, far_in, near, far, mid, later, mass, along_x, along_y)
    reps = lax.axis_size("rep")
    chunks = lax.all_to_all(chunks.reshape(ring, 8 * LIVE, 128), "gz", 0, 0, tiled=True)
    pieces = bins(me, chunks, place, wide, along_z, pieces.reshape(reps, SPAN, 1, 128))
    pieces = lax.all_to_all(pieces, "rep", 0, 0, tiled=True)
    out, sums = pick(item.reshape(-1), pieces.reshape(reps * SPAN, 128))
    got = lax.all_to_all(out.reshape(reps, PER, DEPTH, 128), "rep", 0, 0, tiled=True)
    step = 1
    while step < ring:
        sums = sums + lax.ppermute(sums, "gz", [(i, i ^ step) for i in range(ring)])
        step *= 2
    resampled, propagator = finish(got.reshape(reps * PER, DEPTH, 128), sums)
    return resampled, propagator


def solution(mesh):
    in_specs = (
        P("rep", "gz", None),
        P(None, "rep", "gz", None),
        P("gz", None),
        P(),
        P(),
        P("gz", None, None),
    )
    out_specs = (P("rep", "gz", None), P("rep", None))
    return jax.shard_map(local, mesh=mesh, in_specs=in_specs, out_specs=out_specs, check_vma=False)
```

```python
import jax
import jax.numpy as jnp
import ml_dtypes
import numpy as np
from jax import lax
from jax.experimental import pallas as pl
from jax.experimental.pallas import tpu as pltpu
from jax.sharding import PartitionSpec as P

L = 64
NBINS = 16
LIVE = 3
DEPTH = 4
ROWS = 32
PER = 6
BLOCKS = LIVE + 1
SPAN = LIVE * DEPTH + 1
GRANT = 8 << 20

VMEM = pltpu.VMEM
SMEM = pltpu.SMEM


def split_constant(table):
    table = table.astype(np.float32)
    high = table.astype(ml_dtypes.bfloat16)
    low = (table - high.astype(np.float32)).astype(ml_dtypes.bfloat16)
    return np.stack([high, low])


def real_basis(sine_wave):
    slot = np.arange(L)[:, None]
    site = np.arange(L)[None, :]
    wave = np.where(slot <= L // 2, slot, sine_wave(slot))
    angle = 2.0 * np.pi / L * (wave * site % L)
    basis = np.where(slot <= L // 2, np.cos(angle), np.sin(angle)) * np.sqrt(2.0)
    basis[0] = 1.0
    basis[L // 2] = np.cos(np.pi * np.arange(L))
    return basis / np.sqrt(L)


def tables():
    basis_x = real_basis(lambda slot: slot - L // 2)
    basis_k = real_basis(lambda slot: L - slot)
    along_x = np.einsum("ab,cd,mx->acxdbm", np.eye(2), np.eye(2), basis_x).reshape(256, 256)
    along_y = basis_k.reshape(16, 2, 2, 32, 2).transpose(2, 1, 0, 4, 3).reshape(64, 64)
    along_z = np.einsum("ab,kz->akzb", np.eye(2), basis_k).reshape(128, 128)
    return split_constant(along_x), split_constant(along_y), split_constant(along_z)


def split(value):
    high = value.astype(jnp.bfloat16)
    return high, (value - high.astype(jnp.float32)).astype(jnp.bfloat16)


def dot(a, b):
    return jnp.dot(a, b, preferred_element_type=jnp.float32)


def live_of(counts_ref, base):
    seen = jnp.int32(0)
    live = [jnp.int32(0)] * LIVE
    for j in range(PER):
        alive = counts_ref[base + j] > 0
        for k in range(LIVE):
            live[k] = jnp.where(alive & (seen == k), j, live[k])
        seen = seen + alive.astype(jnp.int32)
    return live


def planes(ref, *at):
    return [ref[(*at, pl.ds(z, ROWS, stride=DEPTH), slice(None))] for z in range(DEPTH)]


def beside(v, lane):
    swapped = pltpu.roll(v, L, axis=1)
    rows = v.shape[0]
    y = swapped + jnp.where(lane < L, pltpu.roll(swapped, 1, axis=0), pltpu.roll(swapped, rows - 1, axis=0))
    inner = lane & (L - 1)
    low = pltpu.roll(jnp.where(inner == L - 1, swapped, v), 1, axis=1)
    high = pltpu.roll(jnp.where(inner == 0, swapped, v), 127, axis=1)
    return y + (low + high)


KICK = float(np.sqrt(np.float32(0.2)))


def update(center, near, mass, noise_now, lane):
    near = near + beside(center, lane)
    return center * (0.4 - 0.1 * mass - 0.05 * (center * center)) + 0.1 * near + KICK * noise_now


def edges_kernel(base_ref, odd_ref, counts_ref, field, noise, masses, near_out, far_out, mid, later, mbuf, fbuf, nbuf, sems):
    odd = odd_ref[0] > 0
    live = live_of(counts_ref, base_ref[0])
    first = pltpu.make_async_copy(masses, mbuf, sems.at[2 * LIVE])
    first.start()
    copies = []
    for k in range(LIVE):
        copies.append(
            [
                pltpu.make_async_copy(field.at[live[k]], fbuf.at[k], sems.at[2 * k]),
                pltpu.make_async_copy(noise.at[0, live[k]], nbuf.at[k], sems.at[2 * k + 1]),
            ]
        )
        for copy in copies[-1]:
            copy.start()
    last = [pltpu.make_async_copy(noise.at[1, live[k]], later.at[k], sems.at[2 * LIVE + 1 + k]) for k in range(LIVE)]
    for copy in last:
        copy.start()
    first.wait()
    lane = lax.broadcasted_iota(jnp.int32, (ROWS, 128), 1)
    mass = planes(mbuf)
    for k in range(LIVE):
        for copy in copies[k]:
            copy.wait()
        old = planes(fbuf, k)
        kicks = planes(nbuf, k)
        near = (old[1], old[0] + old[2], old[1] + old[3], old[2])
        new = [update(old[z], near[z], mass[z], kicks[z], lane) for z in range(DEPTH)]
        for i, value in ((0, old), (1, new)):
            near_out[2 * k + i] = jnp.where(odd, value[0], value[3])
            far_out[2 * k + i] = jnp.where(odd, value[3], value[0])
        mid[2 * k] = new[1]
        mid[2 * k + 1] = new[2]
    for copy in last:
        copy.wait()


def floor_div(value, by):
    return jnp.floor((value.astype(jnp.float32) + 0.5) * (1.0 / by)).astype(jnp.int32)


def plan_kernel(counts_ref, slots_ref, bins_ref, item_ref, wide_ref, map_ref):
    total = counts_ref.shape[1]
    row = lax.broadcasted_iota(jnp.int32, (total, total), 0)
    col = lax.broadcasted_iota(jnp.int32, (total, total), 1)
    number = jnp.broadcast_to(counts_ref[...].astype(jnp.float32), (total, total))
    slot = jnp.broadcast_to(slots_ref[...].astype(jnp.float32), (total, total))

    def along(mask, value):
        return jnp.sum(jnp.where(mask, value, 0.0), axis=1, keepdims=True)

    own = along(row == col, number)
    ends = along(col <= row, number)
    slot_column = along(row == col, slot)
    block_row = floor_div(row, PER)
    block_col = floor_div(col, PER)
    rank = along((block_row == block_col) & (col < row) & (number > 0.0), jnp.ones_like(number))
    name = DEPTH * rank + SPAN * block_row[:, :1].astype(jnp.float32)
    position = jnp.sum(
        jnp.where(slot_column == col.astype(jnp.float32), row.astype(jnp.float32), 0.0), axis=0, keepdims=True
    )
    held = (position >= ends - own) & (position < ends)
    item = jnp.sum(jnp.where(held, name, 0.0), axis=0, keepdims=True)
    item_ref[...] = item.astype(jnp.int32)
    devices = total // PER
    to = lax.broadcasted_iota(jnp.int32, (devices, total), 0)
    s = lax.broadcasted_iota(jnp.int32, (devices, total), 1)
    lane = lax.broadcasted_iota(jnp.int32, (devices, 128), 1)
    wide = jnp.full((devices, 128), -1.0, jnp.float32)
    items = jnp.broadcast_to(item, (devices, total))
    for q in range(PER):
        column = jnp.sum(jnp.where(s == to * PER + q, items, 0.0), axis=1, keepdims=True)
        wide = jnp.where((lane >= NBINS * q) & (lane < NBINS * (q + 1)), column, wide)
    wide_ref[...] = wide.astype(jnp.int32)
    lane = lax.broadcasted_iota(jnp.int32, (L, 128), 1)
    for pair in range(2):
        halves = []
        for odd in range(2):
            bins = bins_ref[2 * pair + odd]
            halves.append(jnp.where(lane <= L // 2, bins, pltpu.roll(bins, L // 2, axis=1)))
        map_ref[pair * L : (pair + 1) * L, :] = jnp.where(lane < L, halves[0], pltpu.roll(halves[1], L, axis=1))


def sweep_kernel(
    odd_ref, near_in, far_in, near_own, far_own, mid, later, masses, along_x, along_y, pieces, chunks
):
    odd = odd_ref[0] > 0
    lane = lax.broadcasted_iota(jnp.int32, (ROWS, 128), 1)
    mass = planes(masses)
    left = []
    for k in range(LIVE):
        beyond = [t[2 * k + 1] + 0.1 * own[2 * k] for t, own in ((near_in, near_own), (far_in, far_own))]
        within = [own[2 * k + 1] + 0.1 * t[2 * k] for t, own in ((near_in, near_own), (far_in, far_own))]
        now = [
            jnp.where(odd, beyond[0], beyond[1]),
            jnp.where(odd, within[0], within[1]),
            mid[2 * k],
            mid[2 * k + 1],
            jnp.where(odd, within[1], within[0]),
            jnp.where(odd, beyond[1], beyond[0]),
        ]
        kicks = planes(later, k)
        new = [update(now[p + 1], now[p] + now[p + 2], mass[p], kicks[p], lane) for p in range(DEPTH)]
        for z in range(DEPTH):
            pieces[pl.ds(k * DEPTH + z, ROWS, stride=SPAN), :] = new[z]
        left += [jnp.concatenate(new[0:2], axis=1), jnp.concatenate(new[2:4], axis=1)]
    high, low = split(jnp.concatenate(left, axis=0))
    across = dot(high, along_x[0]) + (dot(low, along_x[0]) + dot(high, along_x[1]))
    parts = [across[i * ROWS : (i + 1) * ROWS] for i in range(2 * LIVE)]
    right = jnp.concatenate([jnp.concatenate([p[:, :128], p[:, 128:]], axis=0) for p in parts], axis=1)
    high, low = split(right)
    turned = dot(along_y[0], high) + (dot(along_y[0], low) + dot(along_y[1], high))
    for i in range(2 * LIVE):
        even = turned[:ROWS, 128 * i : 128 * (i + 1)]
        odd = turned[ROWS:, 128 * i : 128 * (i + 1)]
        ready = (
            jnp.where(lane < L, even, pltpu.roll(odd, L, axis=1)),
            jnp.where(lane < L, pltpu.roll(even, L, axis=1), odd),
        )
        for side in range(2):
            for pair in range(2):
                chunks[pl.ds(i * 4 + side * 2 + pair, 16, stride=8 * LIVE), :] = ready[side][16 * pair : 16 * pair + 16]


def bins_kernel(me_ref, chunks, map_ref, wide, along_z, old, pieces, rows):
    devices = wide.shape[0]
    place = map_ref[...]
    power = []
    for k in range(LIVE):
        high, low = split(chunks[:, 8 * k : 8 * k + 8, :].reshape(128, 128))
        mode = dot(along_z[0], high) + (dot(along_z[0], low) + dot(along_z[1], high))
        power.append(mode * mode)
    power.append(jnp.ones_like(power[0]))
    for b in range(NBINS):
        here = place == b
        for k in range(BLOCKS):
            rows[k * NBINS + b : k * NBINS + b + 1, :] = jnp.sum(
                jnp.where(here, power[k], 0.0), axis=0, keepdims=True
            )
    rows[BLOCKS * NBINS :, :] = jnp.zeros((128 - BLOCKS * NBINS, 128), jnp.float32)
    sums = lax.dot_general(
        jnp.ones((8, 128), jnp.float32),
        rows[...],
        (((1,), (1,)), ((), ())),
        precision=lax.Precision.HIGHEST,
        preferred_element_type=jnp.float32,
    )[0:1]
    lane = lax.broadcasted_iota(jnp.int32, (1, 128), 1)
    mine = jnp.where(lane >= NBINS * PER, spread(sums, LIVE, lane) * (1.0 / devices), 0.0)
    mine = jnp.broadcast_to(mine, (devices, 128))
    for k in range(LIVE):
        mine = jnp.where(wide[...] == me_ref[0] * SPAN + DEPTH * k, spread(sums, k, lane), mine)
    pieces[...] = old[...]
    pieces[pl.ds(SPAN - 1, devices, stride=SPAN), :] = mine


def spread(row, k, lane):
    row = jnp.where((lane >= NBINS * k) & (lane < NBINS * (k + 1)), row, 0.0)
    for shift in (16, 32, 64):
        row = row + pltpu.roll(row, shift, axis=1)
    return row


def pick_kernel(item_ref, pieces, out, part):
    devices = pieces.shape[0] // SPAN
    for s in range(devices * PER):
        out[s] = pieces[pl.ds(item_ref[s], DEPTH), :]
    part[...] = jnp.sum(pieces[pl.ds(SPAN - 1, devices, stride=SPAN), :], axis=0, keepdims=True)


def finish_kernel(got, sums_ref, resampled, propagator):
    devices = got.shape[0] // PER
    for q in range(PER):
        for d in range(devices):
            resampled[q, :, 128 * d : 128 * (d + 1)] = got[d * PER + q]
    lane = lax.broadcasted_iota(jnp.int32, (1, 128), 1)
    ratio = sums_ref[...] / spread(sums_ref[...], PER, lane)
    for q in range(PER):
        turned = ratio if q == 0 else pltpu.roll(ratio, 128 - NBINS * q, axis=1)
        propagator[q : q + 1, :] = turned[:, :NBINS]


def spec(space):
    return pl.BlockSpec(memory_space=space)


def shape(*dims, dtype=jnp.float32):
    return jax.ShapeDtypeStruct(dims, dtype)


def rows_view(slabs):
    lead = slabs.shape[:-2]
    parts = slabs.reshape(*lead, DEPTH, ROWS, 128)
    return jnp.swapaxes(parts, -3, -2).reshape(*lead, DEPTH * ROWS, 128)


def edges(base, odd, counts, field, noise, masses):
    return pl.pallas_call(
        edges_kernel,
        out_shape=[shape(2 * LIVE, ROWS, 128)] * 3 + [shape(LIVE, 128, 128), shape(128, 128)],
        in_specs=[spec(SMEM)] * 3 + [spec(pl.ANY)] * 3,
        out_specs=[spec(VMEM)] * 5,
        scratch_shapes=[
            VMEM((LIVE, 128, 128), jnp.float32),
            VMEM((LIVE, 128, 128), jnp.float32),
            pltpu.SemaphoreType.DMA((3 * LIVE + 1,)),
        ],
        compiler_params=pltpu.CompilerParams(vmem_limit_bytes=GRANT),
        name="edges",
    )(base, odd, counts, field, noise, masses)


def plan(counts, dest_slots, mode_bins):
    total = counts.shape[0]
    padded = jnp.pad(mode_bins, ((0, 0), (0, 0), (0, 128 - mode_bins.shape[2])))
    return pl.pallas_call(
        plan_kernel,
        out_shape=[
            shape(1, total, dtype=jnp.int32),
            shape(total // PER, 128, dtype=jnp.int32),
            shape(128, 128, dtype=jnp.int32),
        ],
        in_specs=[spec(VMEM)] * 3,
        out_specs=[spec(VMEM)] * 3,
        compiler_params=pltpu.CompilerParams(vmem_limit_bytes=GRANT),
        name="plan",
    )(counts.reshape(1, total), dest_slots.reshape(1, total), padded)


def sweeps(*blocks):
    return pl.pallas_call(
        sweep_kernel,
        out_shape=[shape(ROWS * SPAN, 128), shape(16 * 8 * LIVE, 128)],
        in_specs=[spec(SMEM)] + [spec(VMEM)] * 9,
        out_specs=[spec(VMEM)] * 2,
        compiler_params=pltpu.CompilerParams(vmem_limit_bytes=GRANT),
        name="sweeps",
    )(*blocks)


def bins(me, chunks, place, wide, along_z, pieces):
    devices = wide.shape[0]
    return pl.pallas_call(
        bins_kernel,
        out_shape=shape(devices * SPAN, 128),
        in_specs=[spec(SMEM)] + [spec(VMEM)] * 5,
        out_specs=spec(VMEM),
        scratch_shapes=[VMEM((128, 128), jnp.float32)],
        compiler_params=pltpu.CompilerParams(vmem_limit_bytes=GRANT),
        name="bins",
    )(me, chunks, place, wide, along_z, pieces)


def pick(item, pieces):
    return pl.pallas_call(
        pick_kernel,
        out_shape=[shape(item.shape[0], DEPTH, 128), shape(1, 128)],
        in_specs=[spec(SMEM), spec(VMEM)],
        out_specs=[spec(VMEM)] * 2,
        compiler_params=pltpu.CompilerParams(vmem_limit_bytes=GRANT),
        name="pick",
    )(item, pieces)


def finish(got, sums):
    return pl.pallas_call(
        finish_kernel,
        out_shape=[shape(PER, DEPTH, L * L), shape(PER, NBINS)],
        in_specs=[spec(VMEM)] * 2,
        out_specs=[spec(VMEM)] * 2,
        compiler_params=pltpu.CompilerParams(vmem_limit_bytes=GRANT),
        name="finish",
    )(got, sums)


def local(lattice_field, langevin_noise, masses, counts, dest_slots, mode_bins):
    along_x, along_y, along_z = (jnp.asarray(t) for t in tables())
    me = lax.axis_index("rep").astype(jnp.int32).reshape(1)
    base = me * PER
    field, noise, mass = rows_view(lattice_field), rows_view(langevin_noise), rows_view(masses)
    odd = (lax.axis_index("gz").astype(jnp.int32) & 1).reshape(1)
    held = (pltpu.with_memory_space_constraint(a, pltpu.HBM) for a in (counts, field, noise, mass))
    near, far, mid, later, mass = edges(base, odd, *held)
    ring = lax.axis_size("gz")
    near_in = lax.ppermute(near, "gz", [(i, i ^ 1) for i in range(ring)])
    far_in = lax.ppermute(far, "gz", [(i, (i + 1) % ring if i % 2 else (i - 1) % ring) for i in range(ring)])
    far_in, near_in, item, wide, place = lax.optimization_barrier(
        (far_in, near_in, *plan(counts, dest_slots, mode_bins))
    )
    pieces, chunks = sweeps(odd, near_in, far_in, near, far, mid, later, mass, along_x, along_y)
    reps = lax.axis_size("rep")
    chunks = lax.all_to_all(chunks.reshape(ring, 8 * LIVE, 128), "gz", 0, 0, tiled=True)
    pieces = bins(me, chunks, place, wide, along_z, pieces)
    pieces = lax.all_to_all(pieces.reshape(reps, SPAN, 1, 128), "rep", 0, 0, tiled=True)
    out, sums = pick(item.reshape(-1), pieces.reshape(reps * SPAN, 128))
    got = lax.all_to_all(out.reshape(reps, PER, DEPTH, 128), "rep", 0, 0, tiled=True)
    step = 1
    while step < ring:
        sums = sums + lax.ppermute(sums, "gz", [(i, i ^ step) for i in range(ring)])
        step *= 2
    resampled, propagator = finish(got.reshape(reps * PER, DEPTH, 128), sums)
    return resampled, propagator


def solution(mesh):
    in_specs = (
        P("rep", "gz", None),
        P(None, "rep", "gz", None),
        P("gz", None),
        P(),
        P(),
        P("gz", None, None),
    )
    out_specs = (P("rep", "gz", None), P("rep", None))
    return jax.shard_map(local, mesh=mesh, in_specs=in_specs, out_specs=out_specs, check_vma=False)
```
